512 devices in a mesh: grp: 32 (over z_lo, y, core), tp: 16 (over x, z_hi).
Axes of the slice: x: 4, y: 4, z: 16 (z_hi: 4, z_lo: 4; z = z_hi * 4 + z_lo), core: 2. Of those that a mesh axis runs over, the one named last changes fastest.
Arguments:
- grad_top: bfloat16 [96, 128, 4608], P('grp', None, 'tp'), parts along dimension 0, may hold values from -6 to 6
- post_scale: float32 [128], replicated, may hold values from 0.3 to 3
- post_gain: bfloat16 [4608], P('tp'), may hold values from 0.25 to 1.75
- patterns: bfloat16 [32, 128, 128], P('tp'), may hold values from 0 to 1, as said below
- out_proj: bfloat16 [4096, 4608], P('tp'), may hold values from -0.09375 to 0.09375
- value_proj: bfloat16 [2048, 4608], P('tp'), may hold values from -0.125 to 0.125
- pre_scale: float32 [128], replicated, may hold values from 0.3 to 3
- pre_gain: bfloat16 [4608], P('tp'), may hold values from 0.25 to 1.75
- decoder: bfloat16 [2048, 4608], P('tp'), may hold values from -0.09375 to 0.09375
- block_ids: int32 [128, 2], replicated, may hold values from 0 to 15, all different within a row
- feature_acts: bfloat16 [128, 256], P('tp'), may hold values from 0.099609375 to 4
Outputs:
- attribution: float32 [96, 128, 256], P('grp', 'tp'), parts along dimension 0
The draws below stay inside these ranges and needn't reach their ends.
There are 32 independent parts, one for each index of `grp`. The reference program is written for one: setup_inputs(seed, part) draws one part's arguments, and reference() takes and returns one part's arrays. A program takes and returns all parts, laid end to end along the dimension named above; an argument that names none is the same for every part. Nothing has to cross between parts.
Inputs may be any that keep to these rules, and one draw needn't show every extreme that they name: `block_ids`: each token names 2 different blocks. `patterns`: each query row of each head is zero past its own position and sums to one.
All inputs are finite; a program needn't handle non-finite values.
Results may differ from the reference program's by a relative error of at most 0.019.
Values may be sent and summed in bfloat16 or wider, within the bound.
No kernel may reach another device: no remote copies, remote signals or barrier semaphores. Data moves between devices by JAX's collectives and lax.ppermute only.
A program may use at most 64 MiB of HBM per device.

```python
import math
import jax
import jax.numpy as jnp
from jax import lax

D = 4608
HEADS = 32
KV = 16
HD = 128
BLK = 128
SEQ = 128
SLOTS = 2
TGT = 3
NBLK = 16
KV_DEV = 1


def draw_patterns(key, part):
    key = jax.random.fold_in(key, 7)
    raw = jax.random.uniform(key, (HEADS, SEQ, SEQ), jnp.float32, 0.2, 1.0)
    position = jnp.arange(SEQ)
    causal = (position[:, None] >= position[None, :]).astype(jnp.float32)
    weights = raw * causal[None]
    return (weights / jnp.sum(weights, axis=2, keepdims=True)).astype(jnp.bfloat16)


def levels(key, dims, split, least, largest):
    def one(dim, parts):
        heights = jax.random.uniform(jax.random.fold_in(jax.random.fold_in(key, 6), dim), (parts,), jnp.float32, least / len(split), largest / len(split))
        return jnp.repeat(jnp.exp(heights), dims[dim] // parts).reshape((-1,) + (1,) * (len(dims) - dim - 1))

    gain = one(*split[0])
    for cut in split[1:]:
        gain = gain * one(*cut)
    return gain


def picks_of(stream_key, rows, number_of, top, lift):
    sequence = jax.random.permutation(jax.random.fold_in(stream_key, 1), number_of)
    pull = sequence
    for power in range(3):
        pull = pull * pull // number_of
    pull = pull * lift // number_of
    tickets = jax.random.randint(jax.random.fold_in(stream_key, 2), (rows, number_of), 0, 4096) + pull
    holders = jax.random.permutation(jax.random.fold_in(stream_key, 3), rows)[jnp.arange(number_of) % rows]
    tickets = jnp.where(jnp.arange(rows)[:, None] == holders[None, :], 1 << 14, tickets)
    priority = tickets * number_of + jnp.arange(number_of)
    return lax.top_k(priority.astype(jnp.int32), top)[1].astype(jnp.int32)


def scatter_about(rng, dims, scale, reach, shards=(), kind=jnp.bfloat16):
    loudness = levels(rng, dims, shards, -0.22, 0.18) if shards else 1.0
    drawn = jax.random.normal(rng, dims, jnp.float32) * scale * loudness
    return jnp.minimum(jnp.maximum(drawn, -reach), reach).astype(kind)


def setup_inputs(seed: int = 0, part: int = 0) -> dict:
    splits = jax.random.split(jax.random.key(seed), 12)
    own_keys = jax.random.split(jax.random.fold_in(splits[11], part), 12)
    return {
        "grad_top": scatter_about(own_keys[0], (TGT, SEQ, D), 1.0, 6.0, ((2, 16),)),
        "post_scale": jnp.clip(jnp.exp(jax.random.uniform(splits[1], (SEQ,), jnp.float32, math.log(0.3), math.log(3.0))), 0.3, 3.0),
        "post_gain": jnp.clip(1.0 + 0.15 * jax.random.normal(splits[2], (D,), jnp.float32), 0.25, 1.75).astype(jnp.bfloat16),
        "patterns": draw_patterns(jax.random.fold_in(splits[11], 71), part),
        "out_proj": scatter_about(splits[4], (HEADS * HD, D), D ** -0.5, 0.09375, ((0, 16),)),
        "value_proj": scatter_about(splits[5], (KV * HD, D), (KV * HD) ** -0.5, 0.125, ((0, 16),)),
        "pre_scale": jnp.clip(jnp.exp(jax.random.uniform(splits[6], (SEQ,), jnp.float32, math.log(0.3), math.log(3.0))), 0.3, 3.0),
        "pre_gain": jnp.clip(1.0 + 0.15 * jax.random.normal(splits[7], (D,), jnp.float32), 0.25, 1.75).astype(jnp.bfloat16),
        "decoder": scatter_about(splits[8], (NBLK * BLK, D), D ** -0.5, 0.09375, ((0, 16),)),
        "block_ids": picks_of(splits[9], SEQ, NBLK, SLOTS, 2048),
        "feature_acts": jnp.clip(jnp.exp(math.log(4.0) - 3.6927934 * jax.random.uniform(splits[10], (SEQ, SLOTS * BLK), jnp.float32) ** levels(splits[10], (SEQ, SLOTS * BLK), ((0, 16),), -0.2, 0.2)), 0.099609375, 4.0).astype(jnp.bfloat16),
    }


def reference(grad_top, post_scale, post_gain, patterns, out_proj, value_proj, pre_scale, pre_gain, decoder, block_ids, feature_acts):
    rows = TGT * SEQ
    top = grad_top.astype(jnp.float32)
    scaled = ((top * post_gain.astype(jnp.float32)[None, None, :]) * post_scale[None, :, None]).astype(jnp.bfloat16)
    head_grad = jnp.dot(scaled.reshape(rows, D), out_proj.T, preferred_element_type=jnp.float32).astype(jnp.bfloat16)
    grid = head_grad.reshape(TGT, SEQ, HEADS, HD).astype(jnp.float32)
    mixed = jnp.einsum("hts,rthj->rshj", patterns.astype(jnp.float32), grid)
    value_grad = mixed.reshape(TGT, SEQ, KV, 2, HD).sum(axis=3).astype(jnp.bfloat16).reshape(rows, KV * HD)
    attn_grad = jnp.zeros((rows, D), jnp.float32)
    width = KV_DEV * HD
    for group in range(KV // KV_DEV):
        partial_value = jnp.dot(value_grad[:, group * width:(group + 1) * width], value_proj[group * width:(group + 1) * width], preferred_element_type=jnp.float32)
        attn_grad = attn_grad + partial_value.astype(jnp.bfloat16).astype(jnp.float32)
    pre_rows = jnp.tile(pre_scale, TGT)[:, None]
    bottom = (top.reshape(rows, D) + pre_gain.astype(jnp.float32)[None, :] * pre_rows * attn_grad).astype(jnp.bfloat16)
    scores = jnp.dot(bottom, decoder.T, preferred_element_type=jnp.float32).reshape(TGT, SEQ, NBLK, BLK)
    hit = block_ids[:, :, None] == jnp.arange(NBLK, dtype=jnp.int32)[None, None, :]
    picked = jnp.sum(jnp.where(hit[None, :, :, :, None], scores[:, :, None, :, :], jnp.float32(0.0)), axis=3)
    acts = feature_acts.astype(jnp.float32).reshape(SEQ, SLOTS, BLK)
    return (acts[None] * picked).reshape(TGT, SEQ, SLOTS * BLK)
```

```python
import functools

import jax
import jax.numpy as jnp
from jax import lax
from jax.experimental import pallas as pl
from jax.experimental.pallas import tpu as pltpu
from jax.sharding import Mesh, PartitionSpec as P

BLK = 128
AXES = ("zl", "y", "c", "x", "zh")
GRP = ("zl", "y", "c")
TP = ("x", "zh")
F32 = jnp.float32
BF16 = jnp.bfloat16
PARAMS = pltpu.CompilerParams(vmem_limit_bytes=40 * 1024 * 1024)


def source_block(zh, zl, n):
    return (zh + (n - 1, n - 2, 0, 1)[zl]) % n


def decoder_moves(sizes):
    nzl, ny, nc, nx, nzh = sizes
    senders = (nzl - 1, 2, 1, 0)
    at = lambda zl, y, c, x, zh: (((zl * ny + y) * nc + c) * nx + x) * nzh + zh
    return [
        (at(senders[zl], y, c, x, source_block(zh, zl, nzh)), at(zl, y, c, x, zh))
        for zl in range(nzl)
        for y in range(ny)
        for c in range(nc)
        for x in range(nx)
        for zh in range(nzh)
    ]


def dot(left, right, dims):
    return lax.dot_general(left, right, (dims, ((), ())), preferred_element_type=F32)


def fold_kernel(rows, dec_ref, gain_ref, value_ref, out_ref, acc_ref):
    step = pl.program_id(0)

    @pl.when(step == 0)
    def _():
        acc_ref[...] = jnp.zeros_like(acc_ref)

    gain = gain_ref[0].astype(F32)[0:1]
    wide = dec_ref.shape[2]
    dec = (dec_ref[...].reshape(-1, wide).astype(F32) * gain).astype(BF16)
    acc_ref[...] += dot(dec, value_ref[...], ((1,), (1,)))

    @pl.when(step == pl.num_programs(0) - 1)
    def _():
        out_ref[...] = acc_ref[...].astype(BF16)


def main_kernel(
    geometry,
    blocks_ref,
    x_ref,
    out_proj_ref,
    dec_ref,
    gain_ref,
    post_ref,
    pre_ref,
    patterns_ref,
    ids_ref,
    folded_ref,
    out_ref,
    acc_ref,
    value_ref,
):
    targets, seq, heads, head, nzl, nx, owners = geometry
    step = pl.program_id(0)
    width = heads * head

    @pl.when(step == 0)
    def _():
        acc_ref[...] = jnp.zeros_like(acc_ref)

    gain = gain_ref[0].astype(F32)[0:1]
    proj = (out_proj_ref[...].astype(F32) * gain).astype(BF16)
    left = jnp.concatenate([proj, dec_ref[...]], axis=0)
    acc_ref[...] += dot(left, x_ref[...], ((1,), (0,)))

    @pl.when(step == pl.num_programs(0) - 1)
    def _():
        head_grad = (acc_ref[0:width, :] * post_ref[...]).astype(BF16)
        for r in range(targets):
            cols = slice(r * seq, (r + 1) * seq)
            mixed = jnp.zeros((head, seq), F32)
            for h in range(heads):
                mixed += dot(
                    head_grad[h * head : (h + 1) * head, cols], patterns_ref[h], ((1,), (0,))
                )
            value_ref[cols, :] = mixed.T.astype(BF16)
        value = value_ref[...]
        ids = ids_ref[...]
        slots = ids.shape[1]
        totals = [jnp.zeros((targets * seq, BLK), F32) for _ in range(slots)]
        for zl in range(nzl):
            for x in range(nx):
                rows = folded_ref[zl, :, x].reshape(BLK, head)
                scores = dot(value, rows, ((1,), (1,)))
                name = blocks_ref[zl * nx + x]
                for k in range(slots):
                    totals[k] += jnp.where(ids[:, k : k + 1] == name, scores, 0.0)
        own = blocks_ref[nzl * nx]
        direct = acc_ref[width:, :].T
        for k in range(slots):
            totals[k] = totals[k] * pre_ref[...] + jnp.where(
                ids[:, k : k + 1] == own, direct, 0.0
            )
        piece = seq // owners
        for i in range(owners):
            for r in range(targets):
                lo = r * seq + i * piece
                both = jnp.concatenate([t[lo : lo + piece] for t in totals], axis=0)
                out_ref[i, :, r * BLK : (r + 1) * BLK] = both.astype(BF16)


def last_kernel(targets, parts_ref, acts_ref, out_ref):
    total = jnp.sum(parts_ref[...].astype(F32), axis=0)
    tokens = acts_ref.shape[0]
    slots = acts_ref.shape[1] // BLK
    for r in range(targets):
        for k in range(slots):
            cols = slice(k * BLK, (k + 1) * BLK)
            out_ref[r, :, cols] = (
                total[k * tokens : (k + 1) * tokens, r * BLK : (r + 1) * BLK] * acts_ref[:, cols]
            )


def shards(
    sizes,
    grad_top,
    post_scale,
    post_gain,
    patterns,
    out_proj,
    value_proj,
    pre_scale,
    pre_gain,
    decoder,
    block_ids,
    feature_acts,
):
    nzl, ny, nc, nx, nzh = sizes
    owners = nx * nzh
    targets, seq, local = grad_top.shape
    rows = targets * seq
    heads, head = patterns.shape[0], out_proj.shape[0] // patterns.shape[0]
    width = out_proj.shape[1]
    chunk = width // nx
    slots = block_ids.shape[1]
    copies = ny * nc
    share = BLK // copies
    tokens = feature_acts.shape[0]
    zl, zh, x = lax.axis_index("zl"), lax.axis_index("zh"), lax.axis_index("x")
    copy = lax.axis_index(("y", "c"))

    mine = lax.dynamic_slice_in_dim(decoder, copy * share, share, axis=0)
    near = lax.ppermute(mine, AXES, decoder_moves(sizes))

    turned = grad_top.transpose(2, 0, 1).reshape(local, rows)
    gains = jnp.pad(jnp.stack([post_gain, pre_gain]), ((0, 14), (0, rows - local)))
    columns = lax.all_gather(
        jnp.concatenate([turned, gains], axis=0), "zh", axis=0, tiled=False
    )
    wide = lax.all_gather(columns[:, :local].reshape(chunk, rows), "x", axis=0, tiled=True)

    both = columns[:, local : local + 2, :local].transpose(1, 0, 2).reshape(1, 2 * chunk)
    both = jnp.pad(both, ((0, 15), (0, width - 2 * chunk)))
    near = lax.all_gather(jnp.concatenate([near, both], axis=0), "x", axis=0, tiled=False)

    folded = pl.pallas_call(
        functools.partial(fold_kernel, nx * share),
        grid=(nx,),
        in_specs=[
            pl.BlockSpec((nx, share, chunk), lambda i: (0, 0, i)),
            pl.BlockSpec((1, 16, chunk), lambda i: (i, share // 16, 1)),
            pl.BlockSpec((head, chunk), lambda i: (0, i)),
        ],
        out_specs=pl.BlockSpec((nx * share, head), lambda i: (0, 0)),
        out_shape=jax.ShapeDtypeStruct((nx * share, head), BF16),
        scratch_shapes=[pltpu.VMEM((nx * share, head), F32)],
        compiler_params=PARAMS,
    )(near, near, value_proj)
    folded = lax.all_gather(folded, ("y", "c"), axis=0, tiled=False)
    folded = lax.all_gather(folded, "zl", axis=0, tiled=False)
    folded = folded.reshape(nzl, copies, nx, share, head)

    names = [
        i * nzh + (zh + (nzh - 1, nzh - 2, 0, 1)[j]) % nzh for j in range(nzl) for i in range(nx)
    ]
    names = jnp.stack(names + [x * nzh + zh]).astype(jnp.int32)
    post_row = jnp.tile(post_scale, targets)[None, :]
    pre_col = jnp.tile(pre_scale, targets)[:, None]
    ids = jnp.tile(block_ids, (targets, 1))

    whole = lambda *dims: pl.BlockSpec(dims, lambda i, s: (0,) * len(dims))
    parts = pl.pallas_call(
        functools.partial(main_kernel, (targets, seq, heads, head, nzl, nx, owners)),
        grid_spec=pltpu.PrefetchScalarGridSpec(
            num_scalar_prefetch=1,
            grid=(nx,),
            in_specs=[
                pl.BlockSpec((chunk, rows), lambda i, s: (i, 0)),
                pl.BlockSpec((heads * head, chunk), lambda i, s: (0, i)),
                pl.BlockSpec((BLK, chunk), lambda i, s: (0, i)),
                pl.BlockSpec((1, 16, chunk), lambda i, s: (i, share // 16, 0)),
                whole(1, rows),
                whole(rows, 1),
                whole(heads, seq, seq),
                whole(rows, slots),
                whole(nzl, copies, nx, share, head),
            ],
            out_specs=whole(owners, slots * tokens, targets * BLK),
            scratch_shapes=[
                pltpu.VMEM((heads * head + BLK, rows), F32),
                pltpu.VMEM((rows, head), BF16),
            ],
        ),
        out_shape=jax.ShapeDtypeStruct((owners, slots * tokens, targets * BLK), BF16),
        compiler_params=PARAMS,
    )(names, wide, out_proj, decoder, near, post_row, pre_col, patterns, ids, folded)

    parts = lax.all_to_all(parts, TP, 0, 0)
    return pl.pallas_call(
        functools.partial(last_kernel, targets),
        out_shape=jax.ShapeDtypeStruct((targets, tokens, slots * BLK), F32),
        compiler_params=PARAMS,
    )(parts, feature_acts.astype(F32))


def solution(mesh):
    sizes = (4, 4, mesh.devices.size // 256, 4, 4)
    mesh = Mesh(mesh.devices.reshape(sizes), AXES)
    in_specs = (
        P(GRP, None, TP),
        P(),
        P(TP),
        P(TP, None, None),
        P(TP, None),
        P(TP, None),
        P(),
        P(TP),
        P(TP, None),
        P(),
        P(TP, None),
    )
    return jax.shard_map(
        functools.partial(shards, sizes),
        mesh=mesh,
        in_specs=in_specs,
        out_specs=P(GRP, TP, None),
        check_vma=False,
    )
```

```python
import functools

import jax
import jax.numpy as jnp
from jax import lax
from jax.experimental import pallas as pl
from jax.experimental.pallas import tpu as pltpu
from jax.sharding import Mesh, PartitionSpec as P

BLK = 128
LANES = 128
AXES = ("zl", "y", "c", "x", "zh")
GRP = ("zl", "y", "c")
TP = ("x", "zh")
F32 = jnp.float32
BF16 = jnp.bfloat16
PARAMS = pltpu.CompilerParams(vmem_limit_bytes=40 * 1024 * 1024)
FULL = pltpu.CompilerParams(vmem_limit_bytes=60 * 1024 * 1024)


def source_block(zh, zl, n):
    return (zh + (n - 1, n - 2, 0, 1)[zl]) % n


def decoder_moves(sizes):
    nzl, ny, nc, nx, nzh = sizes
    senders = (nzl - 1, 2, 1, 0)
    at = lambda zl, y, c, x, zh: (((zl * ny + y) * nc + c) * nx + x) * nzh + zh
    return [
        (at(senders[zl], y, c, x, source_block(zh, zl, nzh)), at(zl, y, c, x, zh))
        for zl in range(nzl)
        for y in range(ny)
        for c in range(nc)
        for x in range(nx)
        for zh in range(nzh)
    ]


def ring(size, step):
    return [(i, (i + step) % size) for i in range(size)]


def dot(left, right, dims):
    return lax.dot_general(left, right, (dims, ((), ())), preferred_element_type=F32)


def fold_kernel(dec_ref, value_ref, out_ref, acc_ref):
    step = pl.program_id(0)

    @pl.when(step == 0)
    def _():
        acc_ref[...] = jnp.zeros_like(acc_ref)

    chunk = value_ref.shape[1]
    width = dec_ref.shape[2] - 2 * LANES
    gain = gain_row(dec_ref[step, :, width + LANES : width + 2 * LANES], chunk)
    dec = dec_ref[:, :, pl.ds(pl.multiple_of(step * chunk, LANES), chunk)]
    dec = (dec.reshape(-1, chunk).astype(F32) * gain).astype(BF16)
    acc_ref[...] += dot(dec, value_ref[...], ((1,), (1,)))

    @pl.when(step == pl.num_programs(0) - 1)
    def _():
        out_ref[...] = acc_ref[...].astype(BF16)


def gain_row(tile, chunk):
    tile = tile.astype(F32)
    return jnp.concatenate([tile[i : i + 1] for i in range(chunk // LANES)], axis=1)


def value_kernel(
    geometry,
    order_ref,
    x0,
    x1,
    x2,
    x3,
    out_proj,
    decoder,
    gains_ref,
    post_ref,
    patterns_ref,
    value_ref,
    direct_ref,
    x_buf,
    proj_buf,
    dec_buf,
    sems,
):
    targets, seq, heads, head = geometry
    width = heads * head
    chunk = x_buf.shape[1]
    sources = (x0, x1, x2, x3)
    copies = []
    for n, source in enumerate(sources):
        cols = pl.ds(pl.multiple_of(order_ref[n] * chunk, LANES), chunk)
        group = [
            pltpu.make_async_copy(source, x_buf.at[n], sems.at[0, n]),
            pltpu.make_async_copy(out_proj.at[:, cols], proj_buf.at[n], sems.at[1, n]),
            pltpu.make_async_copy(decoder.at[:, cols], dec_buf.at[n], sems.at[2, n]),
        ]
        for c in group:
            c.start()
        copies.append(group)
    total = None
    for n, group in enumerate(copies):
        for c in group:
            c.wait()
        gain = gain_row(gains_ref[order_ref[n]], chunk)
        proj = (proj_buf[n].astype(F32) * gain).astype(BF16)
        left = jnp.concatenate([proj, dec_buf[n]], axis=0)
        part = dot(left, x_buf[n], ((1,), (0,)))
        total = part if total is None else total + part
    head_grad = (total[0:width] * post_ref[...]).astype(BF16)
    for r in range(targets):
        cols = slice(r * seq, (r + 1) * seq)
        mixed = jnp.zeros((head, seq), F32)
        for h in range(heads):
            mixed += dot(head_grad[h * head : (h + 1) * head, cols], patterns_ref[h], ((1,), (0,)))
        value_ref[cols, :] = mixed.T.astype(BF16)
    direct_ref[...] = total[width:].T


def score_kernel(
    geometry,
    names_ref,
    value_ref,
    direct_ref,
    pre_ref,
    ids_ref,
    m0,
    m1,
    m2,
    m3,
    out_ref,
):
    targets, seq, nx, owners = geometry
    value = value_ref[...]
    head = value.shape[1]
    ids = ids_ref[...]
    slots = ids.shape[1]
    totals = [jnp.zeros((targets * seq, BLK), F32) for _ in range(slots)]
    for n, folded_ref in enumerate((m0, m1, m2, m3)):
        for x in range(nx):
            rows = folded_ref[:, x].reshape(BLK, head)
            scores = dot(value, rows, ((1,), (1,)))
            name = names_ref[n * nx + x]
            for k in range(slots):
                totals[k] += jnp.where(ids[:, k : k + 1] == name, scores, 0.0)
    own = names_ref[4 * nx]
    direct = direct_ref[...]
    for k in range(slots):
        totals[k] = totals[k] * pre_ref[...] + jnp.where(ids[:, k : k + 1] == own, direct, 0.0)
    piece = seq // owners
    for i in range(owners):
        for r in range(targets):
            lo = r * seq + i * piece
            both = jnp.concatenate([t[lo : lo + piece] for t in totals], axis=0)
            out_ref[i, :, r * BLK : (r + 1) * BLK] = both.astype(BF16)


def last_kernel(targets, parts_ref, acts_ref, out_ref):
    total = jnp.sum(parts_ref[...].astype(F32), axis=0)
    tokens = acts_ref.shape[0]
    slots = acts_ref.shape[1] // BLK
    for r in range(targets):
        for k in range(slots):
            cols = slice(k * BLK, (k + 1) * BLK)
            out_ref[r, :, cols] = (
                total[k * tokens : (k + 1) * tokens, r * BLK : (r + 1) * BLK] * acts_ref[:, cols]
            )


def shards(
    sizes,
    grad_top,
    post_scale,
    post_gain,
    patterns,
    out_proj,
    value_proj,
    pre_scale,
    pre_gain,
    decoder,
    block_ids,
    feature_acts,
):
    nzl, ny, nc, nx, nzh = sizes
    owners = nx * nzh
    targets, seq, local = grad_top.shape
    rows = targets * seq
    heads, head = patterns.shape[0], out_proj.shape[0] // patterns.shape[0]
    width = out_proj.shape[1]
    chunk = width // nx
    slots = block_ids.shape[1]
    copies = ny * nc
    share = BLK // copies
    tokens = feature_acts.shape[0]
    zl, zh, x = lax.axis_index("zl"), lax.axis_index("zh"), lax.axis_index("x")
    copy = lax.axis_index(("y", "c"))

    mine = lax.dynamic_slice_in_dim(decoder, copy * share, share, axis=0)
    near = lax.ppermute(mine, AXES, decoder_moves(sizes))

    turned = grad_top.transpose(2, 0, 1).reshape(local, rows)
    gains = jnp.pad(jnp.stack([post_gain, pre_gain]), ((0, 14), (0, rows - local)))
    columns = lax.all_gather(
        jnp.concatenate([turned, gains], axis=0), "zh", axis=0, tiled=False
    )
    tiles = columns[:, local : local + 2, :local].transpose(1, 0, 2).reshape(2, -1, LANES)
    tiles = jnp.pad(tiles, ((0, 0), (0, share - chunk // LANES), (0, 0)))
    near = lax.all_gather(
        jnp.concatenate([near, tiles[0], tiles[1]], axis=1), "x", axis=0, tiled=False
    )
    wide, near = lax.optimization_barrier((columns[:, :local].reshape(chunk, rows), near))
    turns = (0, 1, nx - 1, 2)
    wides = [wide if k == 0 else lax.ppermute(wide, "x", ring(nx, k)) for k in turns]
    order = jnp.stack([(x - k) % nx for k in turns]).astype(jnp.int32)

    folded = pl.pallas_call(
        fold_kernel,
        grid=(nx,),
        in_specs=[
            pl.BlockSpec((nx, share, width + 2 * LANES), lambda i: (0, 0, 0)),
            pl.BlockSpec((head, chunk), lambda i: (0, i)),
        ],
        out_specs=pl.BlockSpec((nx * share, head), lambda i: (0, 0)),
        out_shape=jax.ShapeDtypeStruct((nx * share, head), BF16),
        scratch_shapes=[pltpu.VMEM((nx * share, head), F32)],
        compiler_params=PARAMS,
    )(near, value_proj)
    folded = lax.all_gather(folded, ("y", "c"), axis=0, tiled=False)
    folded = folded.reshape(copies, nx, share, head)
    levels = (0, 1, nzl - 1, 2)
    foldeds = [folded if k == 0 else lax.ppermute(folded, "zl", ring(nzl, k)) for k in levels]
    shifts = jnp.array([nzh - 1, nzh - 2, 0, 1])
    names = [
        i * nzh + (zh + shifts[(zl - k) % nzl]) % nzh for k in levels for i in range(nx)
    ]
    names = jnp.stack(names + [x * nzh + zh]).astype(jnp.int32)
    post_row = jnp.tile(post_scale, targets)[None, :]
    pre_col = jnp.tile(pre_scale, targets)[:, None]
    ids = jnp.tile(block_ids, (targets, 1))

    smem = pl.BlockSpec(memory_space=pltpu.SMEM)
    vmem = pl.BlockSpec(memory_space=pltpu.VMEM)
    hbm = pl.BlockSpec(memory_space=pl.ANY)
    value, direct = pl.pallas_call(
        functools.partial(value_kernel, (targets, seq, heads, head)),
        in_specs=[smem] + [hbm] * 6 + [vmem] * 3,
        out_specs=[vmem, vmem],
        out_shape=[
            jax.ShapeDtypeStruct((rows, head), BF16),
            jax.ShapeDtypeStruct((rows, BLK), F32),
        ],
        scratch_shapes=[
            pltpu.VMEM((nx, chunk, rows), BF16),
            pltpu.VMEM((nx, heads * head, chunk), BF16),
            pltpu.VMEM((nx, BLK, chunk), BF16),
            pltpu.SemaphoreType.DMA((3, nx)),
        ],
        compiler_params=FULL,
    )(
        order,
        *wides,
        out_proj,
        decoder,
        near[:, :, width : width + LANES],
        post_row,
        patterns,
    )
    parts = pl.pallas_call(
        functools.partial(score_kernel, (targets, seq, nx, owners)),
        in_specs=[smem] + [vmem] * 8,
        out_specs=vmem,
        out_shape=jax.ShapeDtypeStruct((owners, slots * tokens, targets * BLK), BF16),
        compiler_params=PARAMS,
    )(names, value, direct, pre_col, ids, *foldeds)

    parts = lax.all_to_all(parts, TP, 0, 0)
    return pl.pallas_call(
        functools.partial(last_kernel, targets),
        out_shape=jax.ShapeDtypeStruct((targets, tokens, slots * BLK), F32),
        compiler_params=PARAMS,
    )(parts, feature_acts.astype(F32))


def solution(mesh):
    sizes = (4, 4, mesh.devices.size // 256, 4, 4)
    mesh = Mesh(mesh.devices.reshape(sizes), AXES)
    in_specs = (
        P(GRP, None, TP),
        P(),
        P(TP),
        P(TP, None, None),
        P(TP, None),
        P(TP, None),
        P(),
        P(TP),
        P(TP, None),
        P(),
        P(TP, None),
    )
    return jax.shard_map(
        functools.partial(shards, sizes),
        mesh=mesh,
        in_specs=in_specs,
        out_specs=P(GRP, TP, None),
        check_vma=False,
    )
```

```python
import functools

import jax
import jax.numpy as jnp
from jax import lax
from jax.experimental import pallas as pl
from jax.experimental.pallas import tpu as pltpu
from jax.sharding import Mesh, PartitionSpec as P

BLK = 128
LANES = 128
AXES = ("zl", "y", "c", "x", "zh")
GRP = ("zl", "y", "c")
TP = ("x", "zh")
TURNS = (0, 2, 1, 3)
F32 = jnp.float32
BF16 = jnp.bfloat16
PARAMS = pltpu.CompilerParams(vmem_limit_bytes=40 * 1024 * 1024)


def source_block(zh, zl, n):
    return (zh + (n - 1, n - 2, 0, 1)[zl]) % n


def decoder_moves(sizes):
    nzl, ny, nc, nx, nzh = sizes
    senders = (nzl - 1, 2, 1, 0)
    at = lambda zl, y, c, x, zh: (((zl * ny + y) * nc + c) * nx + x) * nzh + zh
    return [
        (at(senders[zl], y, c, x, source_block(zh, zl, nzh)), at(zl, y, c, x, zh))
        for zl in range(nzl)
        for y in range(ny)
        for c in range(nc)
        for x in range(nx)
        for zh in range(nzh)
    ]


def ring(size, step):
    return [(i, (i + step) % size) for i in range(size)]


def dot(left, right, dims):
    return lax.dot_general(left, right, (dims, ((), ())), preferred_element_type=F32)


def pack_kernel(top_ref, post_ref, pre_ref, out_ref):
    targets, local, seq = top_ref.shape
    wide = targets * seq
    for r in range(targets):
        out_ref[0:local, r * seq : (r + 1) * seq] = top_ref[r]
    zh = lax.axis_index("zh")
    lane = lax.broadcasted_iota(jnp.int32, (8, wide), 1)
    line = lax.broadcasted_iota(jnp.int32, (8, wide), 0)
    both = []
    for ref in (post_ref, pre_ref):
        flat = jnp.concatenate([ref[...].astype(F32), jnp.zeros((1, wide - local), F32)], axis=1)
        full = jnp.broadcast_to(flat, (8, wide))
        moved = full
        for z in range(1, 4):
            moved = jnp.where(zh == z, pltpu.roll(full, (z * local) % wide, 1), moved)
        place = line * wide + lane - zh * local
        both.append(jnp.where((place >= 0) & (place < local), moved, 0.0))
    out_ref[local:, :] = jnp.concatenate(both, axis=0).astype(BF16)


def join_kernel(columns_ref, wide_ref, gain_ref):
    zone, tall, rows = columns_ref.shape
    local = tall - 16
    total = None
    for z in range(zone):
        wide_ref[z * local : (z + 1) * local] = columns_ref[z, 0:local]
        tail = columns_ref[z, local:].astype(F32)
        total = tail if total is None else total + tail
    gain_ref[...] = total.astype(BF16)


def gain_row(tile, first, count):
    tile = tile.astype(F32)
    return jnp.concatenate([tile[first + i : first + i + 1] for i in range(count)], axis=1)


def fold_kernel(dec_ref, gains_ref, value_ref, out_ref, acc_ref):
    step = pl.program_id(0)

    @pl.when(step == 0)
    def _():
        acc_ref[...] = jnp.zeros_like(acc_ref)

    chunk = value_ref.shape[1]
    gain = gain_row(gains_ref[0], 8, chunk // gains_ref.shape[2])
    dec = (dec_ref[...].reshape(-1, chunk).astype(F32) * gain).astype(BF16)
    acc_ref[...] += dot(dec, value_ref[...], ((1,), (1,)))

    @pl.when(step == pl.num_programs(0) - 1)
    def _():
        out_ref[...] = acc_ref[...].astype(BF16)


def value_kernel(
    geometry,
    own,
    left,
    right,
    low,
    high,
    out_proj,
    decoder,
    near,
    post_ref,
    patterns_ref,
    value_ref,
    direct_ref,
    gains_ref,
    proj_buf,
    dec_buf,
    sem,
    sems,
):
    targets, seq, heads, head = geometry
    width = heads * head
    chunk = proj_buf.shape[2]
    size = 4
    mine = lax.axis_index("x")
    places = [lax.rem(mine + size - turn, size) for turn in (0, 1, 3, 2)]
    tail = pl.ds(decoder.shape[1], gains_ref.shape[2])
    fetch = pltpu.make_async_copy(near.at[:, pl.ds(0, 16), tail], gains_ref, sem)
    fetch.start()
    copies = []
    for n, place in enumerate(places):
        cols = pl.ds(pl.multiple_of(place * chunk, LANES), chunk)
        group = [
            pltpu.make_async_copy(out_proj.at[:, cols], proj_buf.at[n], sems.at[0, n]),
            pltpu.make_async_copy(decoder.at[:, cols], dec_buf.at[n], sems.at[1, n]),
        ]
        for c in group:
            c.start()
        copies.append(group)
    fetch.wait()
    total = None
    for n, sources in enumerate(((own,), (left,), (right,), (low, high))):
        for c in copies[n]:
            c.wait()
        gain = gain_row(gains_ref[places[n]], 0, chunk // gains_ref.shape[2])
        proj = proj_buf[n] * gain.astype(BF16)
        weights = jnp.concatenate([proj, dec_buf[n]], axis=0)
        first = 0
        for source in sources:
            last = first + source.shape[0]
            part = dot(weights[:, first:last], source[...], ((1,), (0,)))
            total = part if total is None else total + part
            first = last
    post = jnp.concatenate([post_ref[...]] * targets, axis=1)
    head_grad = (total[0:width] * post).astype(BF16)
    for r in range(targets):
        cols = slice(r * seq, (r + 1) * seq)
        mixed = jnp.zeros((head, seq), F32)
        for h in range(heads):
            mixed += dot(head_grad[h * head : (h + 1) * head, cols], patterns_ref[h], ((1,), (0,)))
        value_ref[cols, :] = mixed.T.astype(BF16)
    direct_ref[...] = total[width:].T


def score_kernel(geometry, value_ref, direct_ref, pre_ref, ids_ref, m0, m1, m2, m3, out_ref):
    targets, seq, nx, nzh, owners = geometry
    zh, zl = lax.axis_index("zh"), lax.axis_index("zl")
    value = value_ref[...]
    head = value.shape[1]
    slots = ids_ref.shape[0]
    lines = [ids_ref[...].astype(F32), pre_ref[...], jnp.zeros((7 - slots, seq), F32)]
    columns = jnp.concatenate(lines, axis=0).T
    ids = [columns[:, k : k + 1] for k in range(slots)]
    pre = columns[:, slots : slots + 1]
    totals = [[jnp.zeros((seq, BLK), F32) for _ in range(targets)] for _ in range(slots)]
    for turn, folded_ref in zip(TURNS, (m0, m1, m2, m3)):
        other = lax.rem(zl + 4 - turn, 4)
        shift = jnp.where(
            other == 0, nzh - 1, jnp.where(other == 1, nzh - 2, jnp.where(other == 2, 0, 1))
        )
        block = lax.rem(zh + shift, nzh)
        for x in range(nx):
            rows = folded_ref[:, x].reshape(BLK, head)
            scores = dot(value, rows, ((1,), (1,)))
            name = (x * nzh + block).astype(F32)
            for k in range(slots):
                hit = ids[k] == name
                for r in range(targets):
                    totals[k][r] += jnp.where(hit, scores[r * seq : (r + 1) * seq], 0.0)
    own = (lax.axis_index("x") * nzh + zh).astype(F32)
    direct = direct_ref[...]
    for k in range(slots):
        hit = ids[k] == own
        for r in range(targets):
            picked = jnp.where(hit, direct[r * seq : (r + 1) * seq], 0.0)
            totals[k][r] = totals[k][r] * pre + picked
    piece = seq // owners
    for i in range(owners):
        for r in range(targets):
            both = [totals[k][r][i * piece : (i + 1) * piece] for k in range(slots)]
            out_ref[i, :, r * BLK : (r + 1) * BLK] = jnp.concatenate(both, axis=0).astype(BF16)


def last_kernel(targets, parts_ref, acts_ref, out_ref):
    total = jnp.sum(parts_ref[...].astype(F32), axis=0)
    acts = acts_ref[...].astype(F32)
    tokens = acts.shape[0]
    slots = acts.shape[1] // BLK
    for r in range(targets):
        for k in range(slots):
            cols = slice(k * BLK, (k + 1) * BLK)
            out_ref[r, :, cols] = (
                total[k * tokens : (k + 1) * tokens, r * BLK : (r + 1) * BLK] * acts[:, cols]
            )


def shards(
    sizes,
    grad_top,
    post_scale,
    post_gain,
    patterns,
    out_proj,
    value_proj,
    pre_scale,
    pre_gain,
    decoder,
    block_ids,
    feature_acts,
):
    nzl, ny, nc, nx, nzh = sizes
    owners = nx * nzh
    targets, seq, local = grad_top.shape
    rows = targets * seq
    heads, head = patterns.shape[0], out_proj.shape[0] // patterns.shape[0]
    width = out_proj.shape[1]
    chunk = width // nx
    slots = block_ids.shape[1]
    copies = ny * nc
    share = BLK // copies
    tokens = feature_acts.shape[0]
    vmem = pl.BlockSpec(memory_space=pltpu.VMEM)
    hbm = pl.BlockSpec(memory_space=pl.ANY)

    cut = chunk // 2 // LANES * LANES + LANES

    copy = lax.axis_index(("y", "c"))
    near = lax.dynamic_slice_in_dim(decoder, copy * share, share, axis=0)
    near = lax.ppermute(near, AXES, decoder_moves(sizes))
    packed = pl.pallas_call(
        pack_kernel,
        out_shape=jax.ShapeDtypeStruct((local + 16, rows), BF16),
        compiler_params=PARAMS,
    )(grad_top.transpose(0, 2, 1), post_gain[None, :], pre_gain[None, :])
    columns = lax.all_gather(packed, "zh", axis=0, tiled=False)
    wide, gains = pl.pallas_call(
        join_kernel,
        out_shape=[
            jax.ShapeDtypeStruct((chunk, rows), BF16),
            jax.ShapeDtypeStruct((16, rows), BF16),
        ],
        compiler_params=PARAMS,
    )(columns)
    gains = jnp.pad(gains, ((0, share - 16), (0, 0)))
    near = lax.all_gather(jnp.concatenate([near, gains], axis=1), "x", axis=0, tiled=False)
    wide, near = lax.optimization_barrier((wide, near))
    left = lax.ppermute(wide, "x", ring(nx, 1))
    right = lax.ppermute(wide, "x", ring(nx, nx - 1))
    folded = pl.pallas_call(
        fold_kernel,
        grid=(nx,),
        in_specs=[
            pl.BlockSpec((nx, share, chunk), lambda i: (0, 0, i)),
            pl.BlockSpec((1, 16, rows), lambda i: (i, 0, width // rows)),
            pl.BlockSpec((head, chunk), lambda i: (0, i)),
        ],
        out_specs=pl.BlockSpec((nx * share, head), lambda i: (0, 0)),
        out_shape=jax.ShapeDtypeStruct((nx * share, head), BF16),
        scratch_shapes=[pltpu.VMEM((nx * share, head), F32)],
        compiler_params=PARAMS,
    )(near, near, value_proj)
    folded = lax.all_gather(folded, ("y", "c"), axis=0, tiled=False)
    left, right, folded = lax.optimization_barrier((left, right, folded))
    low = lax.ppermute(left[:cut], "x", ring(nx, 1))
    high = lax.ppermute(right[cut:], "x", ring(nx, nx - 1))
    folded = folded.reshape(copies, nx, share, head)
    foldeds = [folded if k == 0 else lax.ppermute(folded, "zl", ring(nzl, k)) for k in TURNS]

    value, direct = pl.pallas_call(
        functools.partial(value_kernel, (targets, seq, heads, head)),
        in_specs=[vmem] * 5 + [hbm] * 3 + [vmem] * 2,
        out_specs=[vmem, vmem],
        out_shape=[
            jax.ShapeDtypeStruct((rows, head), BF16),
            jax.ShapeDtypeStruct((rows, BLK), F32),
        ],
        scratch_shapes=[
            pltpu.VMEM((nx, 16, rows), BF16),
            pltpu.VMEM((nx, heads * head, chunk), BF16),
            pltpu.VMEM((nx, BLK, chunk), BF16),
            pltpu.SemaphoreType.DMA,
            pltpu.SemaphoreType.DMA((2, nx)),
        ],
        compiler_params=PARAMS,
    )(wide, left, right, low, high, out_proj, decoder, near, post_scale[None, :], patterns)
    parts = pl.pallas_call(
        functools.partial(score_kernel, (targets, seq, nx, nzh, owners)),
        out_shape=jax.ShapeDtypeStruct((owners, slots * tokens, targets * BLK), BF16),
        compiler_params=PARAMS,
    )(value, direct, pre_scale[None, :], block_ids.T, *foldeds)

    parts = lax.all_to_all(parts, TP, 0, 0)
    return pl.pallas_call(
        functools.partial(last_kernel, targets),
        out_shape=jax.ShapeDtypeStruct((targets, tokens, slots * BLK), F32),
        compiler_params=PARAMS,
    )(parts, feature_acts)


def solution(mesh):
    sizes = (4, 4, mesh.devices.size // 256, 4, 4)
    mesh = Mesh(mesh.devices.reshape(sizes), AXES)
    in_specs = (
        P(GRP, None, TP),
        P(),
        P(TP),
        P(TP, None, None),
        P(TP, None),
        P(TP, None),
        P(),
        P(TP),
        P(TP, None),
        P(),
        P(TP, None),
    )
    return jax.shard_map(
        functools.partial(shards, sizes),
        mesh=mesh,
        in_specs=in_specs,
        out_specs=P(GRP, TP, None),
        check_vma=False,
    )
```

```python
import functools

import jax
import jax.numpy as jnp
from jax import lax
from jax.experimental import pallas as pl
from jax.experimental.pallas import tpu as pltpu
from jax.sharding import Mesh, PartitionSpec as P

BLK = 128
LANES = 128
AXES = ("zl", "y", "c", "x", "zh")
GRP = ("zl", "y", "c")
TP = ("x", "zh")
TURNS = (0, 2, 1, 3)
F32 = jnp.float32
BF16 = jnp.bfloat16
PARAMS = pltpu.CompilerParams(vmem_limit_bytes=40 * 1024 * 1024)


def source_block(zh, zl, n):
    return (zh + (n - 1, n - 2, 0, 1)[zl]) % n


def decoder_moves(sizes):
    nzl, ny, nc, nx, nzh = sizes
    senders = (nzl - 1, 2, 1, 0)
    at = lambda zl, y, c, x, zh: (((zl * ny + y) * nc + c) * nx + x) * nzh + zh
    return [
        (at(senders[zl], y, c, x, source_block(zh, zl, nzh)), at(zl, y, c, x, zh))
        for zl in range(nzl)
        for y in range(ny)
        for c in range(nc)
        for x in range(nx)
        for zh in range(nzh)
    ]


def ring(size, step):
    return [(i, (i + step) % size) for i in range(size)]


def dot(left, right, dims):
    return lax.dot_general(left, right, (dims, ((), ())), preferred_element_type=F32)


def pack_kernel(top_ref, post_ref, pre_ref, out_ref):
    targets, local, seq = top_ref.shape
    wide = targets * seq
    for r in range(targets):
        out_ref[0:local, r * seq : (r + 1) * seq] = top_ref[r]
    zh = lax.axis_index("zh")
    lane = lax.broadcasted_iota(jnp.int32, (8, wide), 1)
    line = lax.broadcasted_iota(jnp.int32, (8, wide), 0)
    both = []
    for ref in (post_ref, pre_ref):
        flat = jnp.concatenate([ref[...].astype(F32), jnp.zeros((1, wide - local), F32)], axis=1)
        full = jnp.broadcast_to(flat, (8, wide))
        moved = full
        for z in range(1, 4):
            moved = jnp.where(zh == z, pltpu.roll(full, (z * local) % wide, 1), moved)
        place = line * wide + lane - zh * local
        both.append(jnp.where((place >= 0) & (place < local), moved, 0.0))
    out_ref[local:, :] = jnp.concatenate(both, axis=0).astype(BF16)


def join_kernel(columns_ref, wide_ref, gain_ref):
    zone, tall, rows = columns_ref.shape
    local = tall - 16
    total = None
    for z in range(zone):
        wide_ref[z * local : (z + 1) * local] = columns_ref[z, 0:local]
        tail = columns_ref[z, local:].astype(F32)
        total = tail if total is None else total + tail
    gain_ref[...] = total.astype(BF16)


def gain_row(tile, first, count):
    tile = tile.astype(F32)
    return jnp.concatenate([tile[first + i : first + i + 1] for i in range(count)], axis=1)


def fold_kernel(dec_ref, gains_ref, value_ref, out_ref, acc_ref):
    step = pl.program_id(0)

    @pl.when(step == 0)
    def _():
        acc_ref[...] = jnp.zeros_like(acc_ref)

    chunk = value_ref.shape[1]
    gain = gain_row(gains_ref[0], 8, chunk // gains_ref.shape[2])
    dec = (dec_ref[...].reshape(-1, chunk).astype(F32) * gain).astype(BF16)
    acc_ref[...] += dot(dec, value_ref[...], ((1,), (1,)))

    @pl.when(step == pl.num_programs(0) - 1)
    def _():
        out_ref[...] = jnp.broadcast_to(acc_ref[...].astype(BF16)[None], out_ref.shape)


def value_kernel(
    geometry,
    own,
    left,
    right,
    low,
    high,
    out_proj,
    decoder,
    near,
    post_ref,
    patterns_ref,
    value_ref,
    direct_ref,
    gains_ref,
    proj_buf,
    dec_buf,
    sem,
    sems,
):
    targets, seq, heads, head = geometry
    width = heads * head
    chunk = proj_buf.shape[2]
    size = 4
    mine = lax.axis_index("x")
    places = [lax.rem(mine + size - turn, size) for turn in (0, 1, 3, 2)]
    tail = pl.ds(decoder.shape[1], gains_ref.shape[2])
    fetch = pltpu.make_async_copy(near.at[:, pl.ds(0, 16), tail], gains_ref, sem)
    fetch.start()
    copies = []
    for n, place in enumerate(places):
        cols = pl.ds(pl.multiple_of(place * chunk, LANES), chunk)
        group = [
            pltpu.make_async_copy(out_proj.at[:, cols], proj_buf.at[n], sems.at[0, n]),
            pltpu.make_async_copy(decoder.at[:, cols], dec_buf.at[n], sems.at[1, n]),
        ]
        for c in group:
            c.start()
        copies.append(group)
    fetch.wait()
    total = None
    for n, sources in enumerate(((own,), (left,), (right,), (low, high))):
        for c in copies[n]:
            c.wait()
        gain = gain_row(gains_ref[places[n]], 0, chunk // gains_ref.shape[2])
        proj = proj_buf[n] * gain.astype(BF16)
        weights = jnp.concatenate([proj, dec_buf[n]], axis=0)
        first = 0
        for source in sources:
            last = first + source.shape[0]
            part = dot(weights[:, first:last], source[...], ((1,), (0,)))
            total = part if total is None else total + part
            first = last
    post = jnp.concatenate([post_ref[...]] * targets, axis=1)
    head_grad = (total[0:width] * post).astype(BF16)
    for r in range(targets):
        cols = slice(r * seq, (r + 1) * seq)
        mixed = jnp.zeros((head, seq), F32)
        for h in range(heads):
            mixed += dot(head_grad[h * head : (h + 1) * head, cols], patterns_ref[h], ((1,), (0,)))
        value_ref[cols, :] = mixed.T.astype(BF16)
    direct_ref[...] = total[width:].T


def score_kernel(geometry, value_ref, direct_ref, pre_ref, ids_ref, m0, m1, m2, m3, out_ref):
    targets, seq, nx, nzh, owners = geometry
    zh, zl = lax.axis_index("zh"), lax.axis_index("zl")
    value = value_ref[...]
    head = value.shape[1]
    slots = ids_ref.shape[0]
    lines = [ids_ref[...].astype(F32), pre_ref[...], jnp.zeros((7 - slots, seq), F32)]
    columns = jnp.concatenate(lines, axis=0).T
    ids = [columns[:, k : k + 1] for k in range(slots)]
    pre = columns[:, slots : slots + 1]
    totals = [[jnp.zeros((seq, BLK), F32) for _ in range(targets)] for _ in range(slots)]
    for turn, folded_ref in zip(TURNS, (m0, m1, m2, m3)):
        other = lax.rem(zl + 4 - turn, 4)
        shift = jnp.where(
            other == 0, nzh - 1, jnp.where(other == 1, nzh - 2, jnp.where(other == 2, 0, 1))
        )
        block = lax.rem(zh + shift, nzh)
        for x in range(nx):
            rows = folded_ref[:, x].reshape(BLK, head)
            scores = dot(value, rows, ((1,), (1,)))
            name = (x * nzh + block).astype(F32)
            for k in range(slots):
                hit = ids[k] == name
                for r in range(targets):
                    totals[k][r] += jnp.where(hit, scores[r * seq : (r + 1) * seq], 0.0)
    own = (lax.axis_index("x") * nzh + zh).astype(F32)
    direct = direct_ref[...]
    for k in range(slots):
        hit = ids[k] == own
        for r in range(targets):
            picked = jnp.where(hit, direct[r * seq : (r + 1) * seq], 0.0)
            totals[k][r] = totals[k][r] * pre + picked
    piece = seq // owners
    for i in range(owners):
        for r in range(targets):
            both = [totals[k][r][i * piece : (i + 1) * piece] for k in range(slots)]
            out_ref[i, :, r * BLK : (r + 1) * BLK] = jnp.concatenate(both, axis=0).astype(BF16)


def last_kernel(targets, parts_ref, acts_ref, out_ref):
    total = jnp.sum(parts_ref[...].astype(F32), axis=0)
    acts = acts_ref[...].astype(F32)
    tokens = acts.shape[0]
    slots = acts.shape[1] // BLK
    for r in range(targets):
        for k in range(slots):
            cols = slice(k * BLK, (k + 1) * BLK)
            out_ref[r, :, cols] = (
                total[k * tokens : (k + 1) * tokens, r * BLK : (r + 1) * BLK] * acts[:, cols]
            )


def shards(
    sizes,
    grad_top,
    post_scale,
    post_gain,
    patterns,
    out_proj,
    value_proj,
    pre_scale,
    pre_gain,
    decoder,
    block_ids,
    feature_acts,
):
    nzl, ny, nc, nx, nzh = sizes
    owners = nx * nzh
    targets, seq, local = grad_top.shape
    rows = targets * seq
    heads, head = patterns.shape[0], out_proj.shape[0] // patterns.shape[0]
    width = out_proj.shape[1]
    chunk = width // nx
    slots = block_ids.shape[1]
    copies = ny * nc
    share = BLK // copies
    tokens = feature_acts.shape[0]
    vmem = pl.BlockSpec(memory_space=pltpu.VMEM)
    hbm = pl.BlockSpec(memory_space=pl.ANY)

    cut = chunk // 2 // LANES * LANES + LANES

    copy = lax.axis_index(("y", "c"))
    near = lax.dynamic_slice_in_dim(decoder, copy * share, share, axis=0)
    near = lax.ppermute(near, AXES, decoder_moves(sizes))
    packed = pl.pallas_call(
        pack_kernel,
        out_shape=jax.ShapeDtypeStruct((local + 16, rows), BF16),
        compiler_params=PARAMS,
    )(grad_top.transpose(0, 2, 1), post_gain[None, :], pre_gain[None, :])
    columns = lax.all_gather(packed, "zh", axis=0, tiled=False)
    wide, gains = pl.pallas_call(
        join_kernel,
        out_shape=[
            jax.ShapeDtypeStruct((chunk, rows), BF16),
            jax.ShapeDtypeStruct((16, rows), BF16),
        ],
        compiler_params=PARAMS,
    )(columns)
    gains = jnp.pad(gains, ((0, share - 16), (0, 0)))
    near = lax.all_gather(jnp.concatenate([near, gains], axis=1), "x", axis=0, tiled=False)
    wide, near = lax.optimization_barrier((wide, near))
    left = lax.ppermute(wide, "x", ring(nx, 1))
    right = lax.ppermute(wide, "x", ring(nx, nx - 1))
    folded = pl.pallas_call(
        fold_kernel,
        grid=(nx,),
        in_specs=[
            pl.BlockSpec((nx, share, chunk), lambda i: (0, 0, i)),
            pl.BlockSpec((1, 16, rows), lambda i: (i, 0, width // rows)),
            pl.BlockSpec((head, chunk), lambda i: (0, i)),
        ],
        out_specs=pl.BlockSpec((copies, nx * share, head), lambda i: (0, 0, 0)),
        out_shape=jax.ShapeDtypeStruct((copies, nx * share, head), BF16),
        scratch_shapes=[pltpu.VMEM((nx * share, head), F32)],
        compiler_params=PARAMS,
    )(near, near, value_proj)
    folded = lax.all_to_all(folded, ("y", "c"), 0, 0)
    left, right, folded = lax.optimization_barrier((left, right, folded))
    low = lax.ppermute(left[:cut], "x", ring(nx, 1))
    high = lax.ppermute(right[cut:], "x", ring(nx, nx - 1))
    folded = folded.reshape(copies, nx, share, head)
    foldeds = [folded if k == 0 else lax.ppermute(folded, "zl", ring(nzl, k)) for k in TURNS]

    value, direct = pl.pallas_call(
        functools.partial(value_kernel, (targets, seq, heads, head)),
        in_specs=[vmem] * 5 + [hbm] * 3 + [vmem] * 2,
        out_specs=[vmem, vmem],
        out_shape=[
            jax.ShapeDtypeStruct((rows, head), BF16),
            jax.ShapeDtypeStruct((rows, BLK), F32),
        ],
        scratch_shapes=[
            pltpu.VMEM((nx, 16, rows), BF16),
            pltpu.VMEM((nx, heads * head, chunk), BF16),
            pltpu.VMEM((nx, BLK, chunk), BF16),
            pltpu.SemaphoreType.DMA,
            pltpu.SemaphoreType.DMA((2, nx)),
        ],
        compiler_params=PARAMS,
    )(wide, left, right, low, high, out_proj, decoder, near, post_scale[None, :], patterns)
    parts = pl.pallas_call(
        functools.partial(score_kernel, (targets, seq, nx, nzh, owners)),
        out_shape=jax.ShapeDtypeStruct((owners, slots * tokens, targets * BLK), BF16),
        compiler_params=PARAMS,
    )(value, direct, pre_scale[None, :], block_ids.T, *foldeds)

    parts = lax.all_to_all(parts, TP, 0, 0)
    return pl.pallas_call(
        functools.partial(last_kernel, targets),
        out_shape=jax.ShapeDtypeStruct((targets, tokens, slots * BLK), F32),
        compiler_params=PARAMS,
    )(parts, feature_acts)


def solution(mesh):
    sizes = (4, 4, mesh.devices.size // 256, 4, 4)
    mesh = Mesh(mesh.devices.reshape(sizes), AXES)
    in_specs = (
        P(GRP, None, TP),
        P(),
        P(TP),
        P(TP, None, None),
        P(TP, None),
        P(TP, None),
        P(),
        P(TP),
        P(TP, None),
        P(),
        P(TP, None),
    )
    return jax.shard_map(
        functools.partial(shards, sizes),
        mesh=mesh,
        in_specs=in_specs,
        out_specs=P(GRP, TP, None),
        check_vma=False,
    )
```

```python
import functools

import jax
import jax.numpy as jnp
from jax import lax
from jax.experimental import pallas as pl
from jax.experimental.pallas import tpu as pltpu
from jax.sharding import Mesh, PartitionSpec as P

BLK = 128
LANES = 128
AXES = ("zl", "y", "c", "x", "zh")
GRP = ("zl", "y", "c")
TP = ("x", "zh")
TURNS = (0, 1, 3, 2)
ORDER = (2, 3, 0, 1)
F32 = jnp.float32
BF16 = jnp.bfloat16
PARAMS = pltpu.CompilerParams(vmem_limit_bytes=40 * 1024 * 1024)
FULL = pltpu.CompilerParams(vmem_limit_bytes=60 * 1024 * 1024)


def source_block(zh, zl, n):
    return (zh + (n - 1, n - 2, 0, 1)[zl]) % n


def decoder_moves(sizes):
    nzl, ny, nc, nx, nzh = sizes
    senders = (nzl - 1, 2, 1, 0)
    at = lambda zl, y, c, x, zh: (((zl * ny + y) * nc + c) * nx + x) * nzh + zh
    return [
        (at(senders[zl], y, c, x, source_block(zh, zl, nzh)), at(zl, y, c, x, zh))
        for zl in range(nzl)
        for y in range(ny)
        for c in range(nc)
        for x in range(nx)
        for zh in range(nzh)
    ]


def ring(size, step):
    return [(i, (i + step) % size) for i in range(size)]


def dot(left, right, dims):
    return lax.dot_general(left, right, (dims, ((), ())), preferred_element_type=F32)


def front_kernel(share, top, out_proj, dec, post, pre, out_ref, far_ref, near_ref, flat0, flat1, sems):
    targets, local, seq = top.shape
    wide = targets * seq
    height, chunk = out_proj.shape[0], far_ref.shape[1]
    first = pl.multiple_of(lax.rem(lax.axis_index("x") + 2, 4) * chunk, LANES)
    cols = pl.ds(first, chunk)
    copies = [
        pltpu.make_async_copy(post, flat0, sems.at[0]),
        pltpu.make_async_copy(pre, flat1, sems.at[1]),
        pltpu.make_async_copy(out_proj.at[:, cols], far_ref.at[pl.ds(0, height), :], sems.at[2]),
        pltpu.make_async_copy(dec.at[:, cols], far_ref.at[pl.ds(height, BLK), :], sems.at[3]),
    ]
    rows = pl.ds(pl.multiple_of(lax.axis_index(("y", "c")) * share, share), share)
    copies.append(pltpu.make_async_copy(dec.at[rows, :], near_ref, sems.at[4 + targets]))
    for r in range(targets):
        place = out_ref.at[pl.ds(0, local), pl.ds(r * seq, seq)]
        copies.append(pltpu.make_async_copy(top.at[r], place, sems.at[4 + r]))
    for c in copies:
        c.start()
    for c in copies[:2]:
        c.wait()
    zh = lax.axis_index("zh")
    lane = lax.broadcasted_iota(jnp.int32, (8, wide), 1)
    line = lax.broadcasted_iota(jnp.int32, (8, wide), 0)
    both = []
    for ref in (flat0, flat1):
        flat = ref[...].astype(F32).reshape(1, local)
        flat = jnp.concatenate([flat, jnp.zeros((1, wide - local), F32)], axis=1)
        full = jnp.broadcast_to(flat, (8, wide))
        moved = full
        for z in range(1, 4):
            moved = jnp.where(zh == z, pltpu.roll(full, (z * local) % wide, 1), moved)
        place = line * wide + lane - zh * local
        both.append(jnp.where((place >= 0) & (place < local), moved, 0.0))
    out_ref[local:, :] = jnp.concatenate(both, axis=0).astype(BF16)
    for c in copies[2:]:
        c.wait()


def far_kernel(width, wide_ref, weights_ref, gain_ref, out_ref):
    gain = gain_row(gain_ref[...], 0, weights_ref.shape[1] // gain_ref.shape[1])
    proj = weights_ref[0:width] * gain.astype(BF16)
    weights = jnp.concatenate([proj, weights_ref[width:]], axis=0)
    out_ref[...] = dot(weights, wide_ref[...], ((1,), (0,))).astype(BF16)


def join_kernel(columns_ref, wide_ref, gain_ref):
    zone, tall, rows = columns_ref.shape
    local = tall - 16
    total = None
    for z in range(zone):
        wide_ref[z * local : (z + 1) * local] = columns_ref[z, 0:local]
        tail = columns_ref[z, local:].astype(F32)
        total = tail if total is None else total + tail
    gain_ref[...] = total.astype(BF16)


def gain_row(tile, first, count):
    tile = tile.astype(F32)
    return jnp.concatenate([tile[first + i : first + i + 1] for i in range(count)], axis=1)


def fold_kernel(dec_ref, gains_ref, value_ref, out_ref, acc_ref):
    step = pl.program_id(0)

    @pl.when(step == 0)
    def _():
        acc_ref[...] = jnp.zeros_like(acc_ref)

    chunk = value_ref.shape[1]
    gain = gain_row(gains_ref[0], 8, chunk // gains_ref.shape[2])
    dec = (dec_ref[...].reshape(-1, chunk).astype(F32) * gain).astype(BF16)
    acc_ref[...] += dot(dec, value_ref[...], ((1,), (1,)))

    @pl.when(step == pl.num_programs(0) - 1)
    def _():
        out_ref[...] = jnp.broadcast_to(acc_ref[...].astype(BF16)[None], out_ref.shape)


def value_kernel(
    geometry,
    own,
    left,
    right,
    far,
    out_proj,
    decoder,
    near,
    post_ref,
    patterns_ref,
    value_ref,
    direct_ref,
    gains_ref,
    proj_buf,
    dec_buf,
    sem,
    sems,
):
    targets, seq, heads, head = geometry
    width = heads * head
    chunk = proj_buf.shape[2]
    size = 4
    mine = lax.axis_index("x")
    places = [lax.rem(mine + size - turn, size) for turn in (0, 1, 3)]
    tail = pl.ds(decoder.shape[1], gains_ref.shape[2])
    fetch = pltpu.make_async_copy(near.at[:, pl.ds(0, 16), tail], gains_ref, sem)
    fetch.start()
    copies = []
    for n, place in enumerate(places):
        cols = pl.ds(pl.multiple_of(place * chunk, LANES), chunk)
        group = [
            pltpu.make_async_copy(out_proj.at[:, cols], proj_buf.at[n], sems.at[0, n]),
            pltpu.make_async_copy(decoder.at[:, cols], dec_buf.at[n], sems.at[1, n]),
        ]
        for c in group:
            c.start()
        copies.append(group)
    fetch.wait()
    total = far[...].astype(F32)
    for n, source in enumerate((own, left, right)):
        for c in copies[n]:
            c.wait()
        gain = gain_row(gains_ref[places[n]], 0, chunk // gains_ref.shape[2])
        proj = proj_buf[n] * gain.astype(BF16)
        weights = jnp.concatenate([proj, dec_buf[n]], axis=0)
        total += dot(weights, source[...], ((1,), (0,)))
    post = jnp.concatenate([post_ref[...]] * targets, axis=1)
    head_grad = (total[0:width] * post).astype(BF16)
    for r in range(targets):
        cols = slice(r * seq, (r + 1) * seq)
        mixed = jnp.zeros((head, seq), F32)
        for h in range(heads):
            mixed += dot(head_grad[h * head : (h + 1) * head, cols], patterns_ref[h], ((1,), (0,)))
        value_ref[cols, :] = mixed.T.astype(BF16)
    direct_ref[...] = total[width:].T


def score_kernel(geometry, value_ref, direct_ref, pre_ref, ids_ref, m0, m1, m2, m3, out_ref):
    targets, seq, nx, nzh, owners = geometry
    zh, zl = lax.axis_index("zh"), lax.axis_index("zl")
    value = value_ref[...]
    head = value.shape[1]
    slots = ids_ref.shape[0]
    lines = [ids_ref[...].astype(F32), pre_ref[...], jnp.zeros((7 - slots, seq), F32)]
    columns = jnp.concatenate(lines, axis=0).T
    ids = [columns[:, k : k + 1] for k in range(slots)]
    pre = columns[:, slots : slots + 1]
    totals = [[jnp.zeros((seq, BLK), F32) for _ in range(targets)] for _ in range(slots)]
    for turn, folded_ref in zip(TURNS, (m0, m1, m2, m3)):
        other = lax.rem(zl + 4 - turn, 4)
        shift = jnp.where(
            other == 0, nzh - 1, jnp.where(other == 1, nzh - 2, jnp.where(other == 2, 0, 1))
        )
        block = lax.rem(zh + shift, nzh)
        for x in range(nx):
            rows = folded_ref[:, x].reshape(BLK, head)
            scores = dot(value, rows, ((1,), (1,)))
            name = (x * nzh + block).astype(F32)
            for k in range(slots):
                hit = ids[k] == name
                for r in range(targets):
                    totals[k][r] += jnp.where(hit, scores[r * seq : (r + 1) * seq], 0.0)
    own = (lax.axis_index("x") * nzh + zh).astype(F32)
    direct = direct_ref[...]
    for k in range(slots):
        hit = ids[k] == own
        for r in range(targets):
            picked = jnp.where(hit, direct[r * seq : (r + 1) * seq], 0.0)
            totals[k][r] = totals[k][r] * pre + picked
    piece = seq // owners
    for i in range(owners):
        place = ORDER.index(i // nzh) * nzh + ORDER.index(i % nzh)
        for r in range(targets):
            both = [totals[k][r][i * piece : (i + 1) * piece] for k in range(slots)]
            out_ref[place, :, r * BLK : (r + 1) * BLK] = jnp.concatenate(both, axis=0).astype(BF16)


def last_kernel(targets, parts_ref, acts_ref, out_ref):
    total = jnp.sum(parts_ref[...].astype(F32), axis=0)
    acts = acts_ref[...].astype(F32)
    tokens = acts.shape[0]
    slots = acts.shape[1] // BLK
    for r in range(targets):
        for k in range(slots):
            cols = slice(k * BLK, (k + 1) * BLK)
            out_ref[r, :, cols] = (
                total[k * tokens : (k + 1) * tokens, r * BLK : (r + 1) * BLK] * acts[:, cols]
            )


def shards(
    sizes,
    grad_top,
    post_scale,
    post_gain,
    patterns,
    out_proj,
    value_proj,
    pre_scale,
    pre_gain,
    decoder,
    block_ids,
    feature_acts,
):
    nzl, ny, nc, nx, nzh = sizes
    owners = nx * nzh
    targets, seq, local = grad_top.shape
    rows = targets * seq
    heads, head = patterns.shape[0], out_proj.shape[0] // patterns.shape[0]
    width = out_proj.shape[1]
    chunk = width // nx
    slots = block_ids.shape[1]
    copies = ny * nc
    share = BLK // copies
    tokens = feature_acts.shape[0]
    vmem = pl.BlockSpec(memory_space=pltpu.VMEM)
    hbm = pl.BlockSpec(memory_space=pl.ANY)

    packed, weights, near = pl.pallas_call(
        functools.partial(front_kernel, share),
        in_specs=[hbm] * 5,
        out_shape=[
            jax.ShapeDtypeStruct((local + 16, rows), BF16),
            jax.ShapeDtypeStruct((heads * head + BLK, chunk), BF16),
            jax.ShapeDtypeStruct((share, width), BF16),
        ],
        scratch_shapes=[
            pltpu.VMEM((local,), BF16),
            pltpu.VMEM((local,), BF16),
            pltpu.SemaphoreType.DMA((5 + targets,)),
        ],
        compiler_params=FULL,
    )(grad_top.transpose(0, 2, 1), out_proj, decoder, post_gain, pre_gain)
    near = lax.ppermute(near, AXES, decoder_moves(sizes))
    weights = lax.ppermute(weights, "x", ring(nx, 2))
    columns = lax.all_gather(packed, "zh", axis=0, tiled=False)
    wide, gains = pl.pallas_call(
        join_kernel,
        out_shape=[
            jax.ShapeDtypeStruct((chunk, rows), BF16),
            jax.ShapeDtypeStruct((16, rows), BF16),
        ],
        compiler_params=PARAMS,
    )(columns)
    tail = jnp.pad(gains, ((0, share - 16), (0, 0)))
    near = lax.all_gather(jnp.concatenate([near, tail], axis=1), "x", axis=0, tiled=False)
    wide, near = lax.optimization_barrier((wide, near))
    left = lax.ppermute(wide, "x", ring(nx, 1))
    right = lax.ppermute(wide, "x", ring(nx, nx - 1))
    far = pl.pallas_call(
        functools.partial(far_kernel, heads * head),
        out_shape=jax.ShapeDtypeStruct((heads * head + BLK, rows), BF16),
        compiler_params=PARAMS,
    )(wide, weights, gains)
    far = lax.ppermute(far, "x", ring(nx, 2))
    folded = pl.pallas_call(
        fold_kernel,
        grid=(nx,),
        in_specs=[
            pl.BlockSpec((nx, share, chunk), lambda i: (0, 0, i)),
            pl.BlockSpec((1, 16, rows), lambda i: (i, 0, width // rows)),
            pl.BlockSpec((head, chunk), lambda i: (0, i)),
        ],
        out_specs=pl.BlockSpec((copies, nx * share, head), lambda i: (0, 0, 0)),
        out_shape=jax.ShapeDtypeStruct((copies, nx * share, head), BF16),
        scratch_shapes=[pltpu.VMEM((nx * share, head), F32)],
        compiler_params=PARAMS,
    )(near, near, value_proj)
    folded = lax.all_to_all(folded, ("y", "c"), 0, 0)
    folded = folded.reshape(copies, nx, share, head)
    foldeds = [folded if k == 0 else lax.ppermute(folded, "zl", ring(nzl, k)) for k in TURNS]

    value, direct = pl.pallas_call(
        functools.partial(value_kernel, (targets, seq, heads, head)),
        in_specs=[vmem] * 4 + [hbm] * 3 + [vmem] * 2,
        out_specs=[vmem, vmem],
        out_shape=[
            jax.ShapeDtypeStruct((rows, head), BF16),
            jax.ShapeDtypeStruct((rows, BLK), F32),
        ],
        scratch_shapes=[
            pltpu.VMEM((nx, 16, rows), BF16),
            pltpu.VMEM((3, heads * head, chunk), BF16),
            pltpu.VMEM((3, BLK, chunk), BF16),
            pltpu.SemaphoreType.DMA,
            pltpu.SemaphoreType.DMA((2, 3)),
        ],
        compiler_params=PARAMS,
    )(wide, left, right, far, out_proj, decoder, near, post_scale[None, :], patterns)
    parts = pl.pallas_call(
        functools.partial(score_kernel, (targets, seq, nx, nzh, owners)),
        out_shape=jax.ShapeDtypeStruct((owners, slots * tokens, targets * BLK), BF16),
        compiler_params=PARAMS,
    )(value, direct, pre_scale[None, :], block_ids.T, *foldeds)

    group = [i * nzh + z for i in ORDER for z in ORDER]
    parts = lax.all_to_all(parts, TP, 0, 0, axis_index_groups=[group])
    return pl.pallas_call(
        functools.partial(last_kernel, targets),
        out_shape=jax.ShapeDtypeStruct((targets, tokens, slots * BLK), F32),
        compiler_params=PARAMS,
    )(parts, feature_acts)


def solution(mesh):
    sizes = (4, 4, mesh.devices.size // 256, 4, 4)
    mesh = Mesh(mesh.devices.reshape(sizes), AXES)
    in_specs = (
        P(GRP, None, TP),
        P(),
        P(TP),
        P(TP, None, None),
        P(TP, None),
        P(TP, None),
        P(),
        P(TP),
        P(TP, None),
        P(),
        P(TP, None),
    )
    return jax.shard_map(
        functools.partial(shards, sizes),
        mesh=mesh,
        in_specs=in_specs,
        out_specs=P(GRP, TP, None),
        check_vma=False,
    )
```

```python
import functools

import jax
import jax.numpy as jnp
from jax import lax
from jax.experimental import pallas as pl
from jax.experimental.pallas import tpu as pltpu
from jax.sharding import Mesh, PartitionSpec as P

BLK = 128
LANES = 128
AXES = ("zl", "y", "c", "x", "zh")
GRP = ("zl", "y", "c")
TP = ("x", "zh")
TURNS = (0, 1, 3, 2)
ORDER = (2, 3, 0, 1)
F32 = jnp.float32
BF16 = jnp.bfloat16
PARAMS = pltpu.CompilerParams(vmem_limit_bytes=40 * 1024 * 1024)
FULL = pltpu.CompilerParams(vmem_limit_bytes=60 * 1024 * 1024)


def source_block(zh, zl, n):
    return (zh + (n - 1, 0, 2, 1)[zl]) % n


def decoder_moves(sizes):
    nzl, ny, nc, nx, nzh = sizes
    senders = (nzl - 1, 2, 1, 0)
    at = lambda zl, y, c, x, zh: (((zl * ny + y) * nc + c) * nx + x) * nzh + zh
    return [
        (at(senders[zl], y, c, x, source_block(zh, zl, nzh)), at(zl, y, c, x, zh))
        for zl in range(nzl)
        for y in range(ny)
        for c in range(nc)
        for x in range(nx)
        for zh in range(nzh)
    ]


def ring(size, step):
    return [(i, (i + step) % size) for i in range(size)]


def dot(left, right, dims):
    return lax.dot_general(left, right, (dims, ((), ())), preferred_element_type=F32)


def front_kernel(share, top, out_proj, dec, post, pre, out_ref, far_ref, near_ref, flat0, flat1, sems):
    targets, local, seq = top.shape
    wide = targets * seq
    height, chunk = out_proj.shape[0], far_ref.shape[1]
    first = pl.multiple_of(lax.rem(lax.axis_index("x") + 2, 4) * chunk, LANES)
    cols = pl.ds(first, chunk)
    copies = [
        pltpu.make_async_copy(post, flat0, sems.at[0]),
        pltpu.make_async_copy(pre, flat1, sems.at[1]),
        pltpu.make_async_copy(out_proj.at[:, cols], far_ref.at[pl.ds(0, height), :], sems.at[2]),
        pltpu.make_async_copy(dec.at[:, cols], far_ref.at[pl.ds(height, BLK), :], sems.at[3]),
    ]
    rows = pl.ds(pl.multiple_of(lax.axis_index(("y", "c")) * share, share), share)
    copies.append(pltpu.make_async_copy(dec.at[rows, :], near_ref, sems.at[4 + targets]))
    for r in range(targets):
        place = out_ref.at[pl.ds(0, local), pl.ds(r * seq, seq)]
        copies.append(pltpu.make_async_copy(top.at[r], place, sems.at[4 + r]))
    for c in copies:
        c.start()
    for c in copies[:2]:
        c.wait()
    zh = lax.axis_index("zh")
    lane = lax.broadcasted_iota(jnp.int32, (8, wide), 1)
    line = lax.broadcasted_iota(jnp.int32, (8, wide), 0)
    both = []
    for ref in (flat0, flat1):
        flat = ref[...].astype(F32).reshape(1, local)
        flat = jnp.concatenate([flat, jnp.zeros((1, wide - local), F32)], axis=1)
        full = jnp.broadcast_to(flat, (8, wide))
        moved = full
        for z in range(1, 4):
            moved = jnp.where(zh == z, pltpu.roll(full, (z * local) % wide, 1), moved)
        place = line * wide + lane - zh * local
        both.append(jnp.where((place >= 0) & (place < local), moved, 0.0))
    out_ref[local:, :] = jnp.concatenate(both, axis=0).astype(BF16)
    for c in copies[2:]:
        c.wait()


def far_kernel(width, wide_ref, weights_ref, gain_ref, out_ref):
    gain = gain_row(gain_ref[...], 0, weights_ref.shape[1] // gain_ref.shape[1])
    proj = weights_ref[0:width] * gain.astype(BF16)
    weights = jnp.concatenate([proj, weights_ref[width:]], axis=0)
    out_ref[...] = dot(weights, wide_ref[...], ((1,), (0,))).astype(BF16)


def join_kernel(columns_ref, wide_ref, gain_ref):
    zone, tall, rows = columns_ref.shape
    local = tall - 16
    total = None
    for z in range(zone):
        wide_ref[z * local : (z + 1) * local] = columns_ref[z, 0:local]
        tail = columns_ref[z, local:].astype(F32)
        total = tail if total is None else total + tail
    gain_ref[...] = total.astype(BF16)


def gain_row(tile, first, count):
    tile = tile.astype(F32)
    return jnp.concatenate([tile[first + i : first + i + 1] for i in range(count)], axis=1)


def fold_kernel(dec_ref, gains_ref, value_ref, out_ref, acc_ref):
    step = pl.program_id(0)

    @pl.when(step == 0)
    def _():
        acc_ref[...] = jnp.zeros_like(acc_ref)

    chunk = value_ref.shape[1]
    gain = gain_row(gains_ref[0], 8, chunk // gains_ref.shape[2])
    dec = (dec_ref[...].reshape(-1, chunk).astype(F32) * gain).astype(BF16)
    acc_ref[...] += dot(dec, value_ref[...], ((1,), (1,)))

    @pl.when(step == pl.num_programs(0) - 1)
    def _():
        out_ref[...] = jnp.broadcast_to(acc_ref[...].astype(BF16)[None], out_ref.shape)


def value_kernel(
    geometry,
    own,
    left,
    right,
    far,
    out_proj,
    decoder,
    near,
    post_ref,
    patterns_ref,
    value_ref,
    direct_ref,
    gains_ref,
    proj_buf,
    dec_buf,
    sem,
    sems,
):
    targets, seq, heads, head = geometry
    width = heads * head
    chunk = proj_buf.shape[2]
    size = 4
    mine = lax.axis_index("x")
    places = [lax.rem(mine + size - turn, size) for turn in (0, 1, 3)]
    tail = pl.ds(decoder.shape[1], gains_ref.shape[2])
    fetch = pltpu.make_async_copy(near.at[:, pl.ds(0, 16), tail], gains_ref, sem)
    fetch.start()
    copies = []
    for n, place in enumerate(places):
        cols = pl.ds(pl.multiple_of(place * chunk, LANES), chunk)
        group = [
            pltpu.make_async_copy(out_proj.at[:, cols], proj_buf.at[n], sems.at[0, n]),
            pltpu.make_async_copy(decoder.at[:, cols], dec_buf.at[n], sems.at[1, n]),
        ]
        for c in group:
            c.start()
        copies.append(group)
    fetch.wait()
    total = far[...].astype(F32)
    for n, source in enumerate((own, left, right)):
        for c in copies[n]:
            c.wait()
        gain = gain_row(gains_ref[places[n]], 0, chunk // gains_ref.shape[2])
        proj = proj_buf[n] * gain.astype(BF16)
        weights = jnp.concatenate([proj, dec_buf[n]], axis=0)
        total += dot(weights, source[...], ((1,), (0,)))
    post = jnp.concatenate([post_ref[...]] * targets, axis=1)
    head_grad = (total[0:width] * post).astype(BF16)
    for r in range(targets):
        cols = slice(r * seq, (r + 1) * seq)
        mixed = jnp.zeros((head, seq), F32)
        for h in range(heads):
            mixed += dot(head_grad[h * head : (h + 1) * head, cols], patterns_ref[h], ((1,), (0,)))
        value_ref[cols, :] = mixed.T.astype(BF16)
    direct_ref[...] = total[width:].T


def score_kernel(geometry, value_ref, direct_ref, pre_ref, ids_ref, m0, m1, m2, m3, out_ref):
    targets, seq, nx, nzh, owners = geometry
    zh, zl = lax.axis_index("zh"), lax.axis_index("zl")
    value = value_ref[...]
    head = value.shape[1]
    slots = ids_ref.shape[0]
    lines = [ids_ref[...].astype(F32), pre_ref[...], jnp.zeros((7 - slots, seq), F32)]
    columns = jnp.concatenate(lines, axis=0).T
    ids = [columns[:, k : k + 1] for k in range(slots)]
    pre = columns[:, slots : slots + 1]
    totals = [[jnp.zeros((seq, BLK), F32) for _ in range(targets)] for _ in range(slots)]
    for turn, folded_ref in zip(TURNS, (m0, m1, m2, m3)):
        other = lax.rem(zl + 4 - turn, 4)
        shift = jnp.where(
            other == 0, nzh - 1, jnp.where(other == 1, 0, jnp.where(other == 2, 2, 1))
        )
        block = lax.rem(zh + shift, nzh)
        for x in range(nx):
            rows = folded_ref[:, x].reshape(BLK, head)
            scores = dot(value, rows, ((1,), (1,)))
            name = (x * nzh + block).astype(F32)
            for k in range(slots):
                hit = ids[k] == name
                for r in range(targets):
                    totals[k][r] += jnp.where(hit, scores[r * seq : (r + 1) * seq], 0.0)
    own = (lax.axis_index("x") * nzh + zh).astype(F32)
    direct = direct_ref[...]
    for k in range(slots):
        hit = ids[k] == own
        for r in range(targets):
            picked = jnp.where(hit, direct[r * seq : (r + 1) * seq], 0.0)
            totals[k][r] = totals[k][r] * pre + picked
    piece = seq // owners
    for i in range(owners):
        place = ORDER.index(i // nzh) * nzh + ORDER.index(i % nzh)
        for r in range(targets):
            both = [totals[k][r][i * piece : (i + 1) * piece] for k in range(slots)]
            out_ref[place, :, r * BLK : (r + 1) * BLK] = jnp.concatenate(both, axis=0).astype(BF16)


def last_kernel(targets, parts_ref, acts_ref, out_ref):
    total = jnp.sum(parts_ref[...].astype(F32), axis=0)
    acts = acts_ref[...].astype(F32)
    tokens = acts.shape[0]
    slots = acts.shape[1] // BLK
    for r in range(targets):
        for k in range(slots):
            cols = slice(k * BLK, (k + 1) * BLK)
            out_ref[r, :, cols] = (
                total[k * tokens : (k + 1) * tokens, r * BLK : (r + 1) * BLK] * acts[:, cols]
            )


def shards(
    sizes,
    grad_top,
    post_scale,
    post_gain,
    patterns,
    out_proj,
    value_proj,
    pre_scale,
    pre_gain,
    decoder,
    block_ids,
    feature_acts,
):
    nzl, ny, nc, nx, nzh = sizes
    owners = nx * nzh
    targets, seq, local = grad_top.shape
    rows = targets * seq
    heads, head = patterns.shape[0], out_proj.shape[0] // patterns.shape[0]
    width = out_proj.shape[1]
    chunk = width // nx
    slots = block_ids.shape[1]
    copies = ny * nc
    share = BLK // copies
    tokens = feature_acts.shape[0]
    vmem = pl.BlockSpec(memory_space=pltpu.VMEM)
    hbm = pl.BlockSpec(memory_space=pl.ANY)

    packed, weights, near = pl.pallas_call(
        functools.partial(front_kernel, share),
        in_specs=[hbm] * 5,
        out_shape=[
            jax.ShapeDtypeStruct((local + 16, rows), BF16),
            jax.ShapeDtypeStruct((heads * head + BLK, chunk), BF16),
            jax.ShapeDtypeStruct((share, width), BF16),
        ],
        scratch_shapes=[
            pltpu.VMEM((local,), BF16),
            pltpu.VMEM((local,), BF16),
            pltpu.SemaphoreType.DMA((5 + targets,)),
        ],
        compiler_params=FULL,
    )(grad_top.transpose(0, 2, 1), out_proj, decoder, post_gain, pre_gain)
    near = lax.ppermute(near, AXES, decoder_moves(sizes))
    weights = lax.ppermute(weights, "x", ring(nx, 2))
    columns = lax.all_gather(packed, "zh", axis=0, tiled=False)
    wide, gains = pl.pallas_call(
        join_kernel,
        out_shape=[
            jax.ShapeDtypeStruct((chunk, rows), BF16),
            jax.ShapeDtypeStruct((16, rows), BF16),
        ],
        compiler_params=PARAMS,
    )(columns)
    tail = jnp.pad(gains, ((0, share - 16), (0, 0)))
    near = lax.all_gather(jnp.concatenate([near, tail], axis=1), "x", axis=0, tiled=False)
    wide, near = lax.optimization_barrier((wide, near))
    left = lax.ppermute(wide, "x", ring(nx, 1))
    right = lax.ppermute(wide, "x", ring(nx, nx - 1))
    far = pl.pallas_call(
        functools.partial(far_kernel, heads * head),
        out_shape=jax.ShapeDtypeStruct((heads * head + BLK, rows), BF16),
        compiler_params=PARAMS,
    )(wide, weights, gains)
    far = lax.ppermute(far, "x", ring(nx, 2))
    folded = pl.pallas_call(
        fold_kernel,
        grid=(nx,),
        in_specs=[
            pl.BlockSpec((nx, share, chunk), lambda i: (0, 0, i)),
            pl.BlockSpec((1, 16, rows), lambda i: (i, 0, width // rows)),
            pl.BlockSpec((head, chunk), lambda i: (0, i)),
        ],
        out_specs=pl.BlockSpec((copies, nx * share, head), lambda i: (0, 0, 0)),
        out_shape=jax.ShapeDtypeStruct((copies, nx * share, head), BF16),
        scratch_shapes=[pltpu.VMEM((nx * share, head), F32)],
        compiler_params=PARAMS,
    )(near, near, value_proj)
    folded = lax.all_to_all(folded, ("y", "c"), 0, 0)
    folded = folded.reshape(copies, nx, share, head)
    foldeds = [folded if k == 0 else lax.ppermute(folded, "zl", ring(nzl, k)) for k in TURNS]

    value, direct = pl.pallas_call(
        functools.partial(value_kernel, (targets, seq, heads, head)),
        in_specs=[vmem] * 4 + [hbm] * 3 + [vmem] * 2,
        out_specs=[vmem, vmem],
        out_shape=[
            jax.ShapeDtypeStruct((rows, head), BF16),
            jax.ShapeDtypeStruct((rows, BLK), F32),
        ],
        scratch_shapes=[
            pltpu.VMEM((nx, 16, rows), BF16),
            pltpu.VMEM((3, heads * head, chunk), BF16),
            pltpu.VMEM((3, BLK, chunk), BF16),
            pltpu.SemaphoreType.DMA,
            pltpu.SemaphoreType.DMA((2, 3)),
        ],
        compiler_params=PARAMS,
    )(wide, left, right, far, out_proj, decoder, near, post_scale[None, :], patterns)
    parts = pl.pallas_call(
        functools.partial(score_kernel, (targets, seq, nx, nzh, owners)),
        out_shape=jax.ShapeDtypeStruct((owners, slots * tokens, targets * BLK), BF16),
        compiler_params=PARAMS,
    )(value, direct, pre_scale[None, :], block_ids.T, *foldeds)

    group = [i * nzh + z for i in ORDER for z in ORDER]
    parts = lax.all_to_all(parts, TP, 0, 0, axis_index_groups=[group])
    return pl.pallas_call(
        functools.partial(last_kernel, targets),
        out_shape=jax.ShapeDtypeStruct((targets, tokens, slots * BLK), F32),
        compiler_params=PARAMS,
    )(parts, feature_acts)


def solution(mesh):
    sizes = (4, 4, mesh.devices.size // 256, 4, 4)
    mesh = Mesh(mesh.devices.reshape(sizes), AXES)
    in_specs = (
        P(GRP, None, TP),
        P(),
        P(TP),
        P(TP, None, None),
        P(TP, None),
        P(TP, None),
        P(),
        P(TP),
        P(TP, None),
        P(),
        P(TP, None),
    )
    return jax.shard_map(
        functools.partial(shards, sizes),
        mesh=mesh,
        in_specs=in_specs,
        out_specs=P(GRP, TP, None),
        check_vma=False,
    )
```

```python
import functools

import jax
import jax.numpy as jnp
from jax import lax
from jax.experimental import pallas as pl
from jax.experimental.pallas import tpu as pltpu
from jax.sharding import Mesh, PartitionSpec as P

BLK = 128
LANES = 128
AXES = ("zl", "y", "c", "x", "zh")
GRP = ("zl", "y", "c")
TP = ("x", "zh")
TURNS = (0, 1, 3, 2)
ORDER = (2, 3, 0, 1)
F32 = jnp.float32
BF16 = jnp.bfloat16
PARAMS = pltpu.CompilerParams(vmem_limit_bytes=40 * 1024 * 1024)
FULL = pltpu.CompilerParams(vmem_limit_bytes=60 * 1024 * 1024)


def source_block(zh, zl, n):
    return (zh + (n - 1, 0, 2, 1)[zl]) % n


def decoder_moves(sizes):
    nzl, ny, nc, nx, nzh = sizes
    senders = (nzl - 1, 2, 1, 0)
    at = lambda zl, y, c, x, zh: (((zl * ny + y) * nc + c) * nx + x) * nzh + zh
    return [
        (at(senders[zl], y, c, x, source_block(zh, zl, nzh)), at(zl, y, c, x, zh))
        for zl in range(nzl)
        for y in range(ny)
        for c in range(nc)
        for x in range(nx)
        for zh in range(nzh)
    ]


def ring(size, step):
    return [(i, (i + step) % size) for i in range(size)]


def dot(left, right, dims):
    return lax.dot_general(left, right, (dims, ((), ())), preferred_element_type=F32)


def front_kernel(share, top, out_proj, dec, post, pre, out_ref, far_ref, near_ref, flat0, flat1, sems):
    targets, local, seq = top.shape
    wide = targets * seq
    height, chunk = out_proj.shape[0], far_ref.shape[1]
    first = pl.multiple_of(lax.rem(lax.axis_index("x") + 2, 4) * chunk, LANES)
    cols = pl.ds(first, chunk)
    copies = [
        pltpu.make_async_copy(post, flat0, sems.at[0]),
        pltpu.make_async_copy(pre, flat1, sems.at[1]),
        pltpu.make_async_copy(out_proj.at[:, cols], far_ref.at[pl.ds(0, height), :], sems.at[2]),
        pltpu.make_async_copy(dec.at[:, cols], far_ref.at[pl.ds(height, BLK), :], sems.at[3]),
    ]
    rows = pl.ds(pl.multiple_of(lax.axis_index(("c", "y")) * share, share), share)
    copies.append(pltpu.make_async_copy(dec.at[rows, :], near_ref, sems.at[4 + targets]))
    for r in range(targets):
        place = out_ref.at[pl.ds(0, local), pl.ds(r * seq, seq)]
        copies.append(pltpu.make_async_copy(top.at[r], place, sems.at[4 + r]))
    for c in copies:
        c.start()
    for c in copies[:2]:
        c.wait()
    zh = lax.axis_index("zh")
    lane = lax.broadcasted_iota(jnp.int32, (8, wide), 1)
    line = lax.broadcasted_iota(jnp.int32, (8, wide), 0)
    both = []
    for ref in (flat0, flat1):
        flat = ref[...].astype(F32).reshape(1, local)
        flat = jnp.concatenate([flat, jnp.zeros((1, wide - local), F32)], axis=1)
        full = jnp.broadcast_to(flat, (8, wide))
        moved = full
        for z in range(1, 4):
            moved = jnp.where(zh == z, pltpu.roll(full, (z * local) % wide, 1), moved)
        place = line * wide + lane - zh * local
        both.append(jnp.where((place >= 0) & (place < local), moved, 0.0))
    out_ref[local:, :] = jnp.concatenate(both, axis=0).astype(BF16)
    for c in copies[2:]:
        c.wait()


def far_kernel(width, wide_ref, weights_ref, gain_ref, out_ref):
    gain = gain_row(gain_ref[...], 0, weights_ref.shape[1] // gain_ref.shape[1])
    proj = weights_ref[0:width] * gain.astype(BF16)
    weights = jnp.concatenate([proj, weights_ref[width:]], axis=0)
    out_ref[...] = dot(weights, wide_ref[...], ((1,), (0,))).astype(BF16)


def join_kernel(columns_ref, wide_ref, gain_ref):
    zone, tall, rows = columns_ref.shape
    local = tall - 16
    total = None
    for z in range(zone):
        wide_ref[z * local : (z + 1) * local] = columns_ref[z, 0:local]
        tail = columns_ref[z, local:].astype(F32)
        total = tail if total is None else total + tail
    gain_ref[...] = total.astype(BF16)


def gain_row(tile, first, count):
    tile = tile.astype(F32)
    return jnp.concatenate([tile[first + i : first + i + 1] for i in range(count)], axis=1)


def fold_kernel(dec_ref, gains_ref, value_ref, out_ref, acc_ref):
    step = pl.program_id(0)

    @pl.when(step == 0)
    def _():
        acc_ref[...] = jnp.zeros_like(acc_ref)

    chunk = value_ref.shape[1]
    gain = gain_row(gains_ref[0], 8, chunk // gains_ref.shape[2])
    dec = (dec_ref[...].reshape(-1, chunk).astype(F32) * gain).astype(BF16)
    acc_ref[...] += dot(dec, value_ref[...], ((1,), (1,)))

    @pl.when(step == pl.num_programs(0) - 1)
    def _():
        out_ref[...] = jnp.broadcast_to(acc_ref[...].astype(BF16)[None], out_ref.shape)


def value_kernel(
    geometry,
    own,
    left,
    right,
    far,
    out_proj,
    decoder,
    near,
    post_ref,
    patterns_ref,
    value_ref,
    direct_ref,
    gains_ref,
    proj_buf,
    dec_buf,
    sem,
    sems,
):
    targets, seq, heads, head = geometry
    width = heads * head
    chunk = proj_buf.shape[2]
    size = 4
    mine = lax.axis_index("x")
    places = [lax.rem(mine + size - turn, size) for turn in (0, 1, 3)]
    tail = pl.ds(decoder.shape[1], gains_ref.shape[2])
    fetch = pltpu.make_async_copy(near.at[:, pl.ds(0, 16), tail], gains_ref, sem)
    fetch.start()
    copies = []
    for n, place in enumerate(places):
        cols = pl.ds(pl.multiple_of(place * chunk, LANES), chunk)
        group = [
            pltpu.make_async_copy(out_proj.at[:, cols], proj_buf.at[n], sems.at[0, n]),
            pltpu.make_async_copy(decoder.at[:, cols], dec_buf.at[n], sems.at[1, n]),
        ]
        for c in group:
            c.start()
        copies.append(group)
    fetch.wait()
    total = far[...].astype(F32)
    for n, source in enumerate((own, left, right)):
        for c in copies[n]:
            c.wait()
        gain = gain_row(gains_ref[places[n]], 0, chunk // gains_ref.shape[2])
        proj = proj_buf[n] * gain.astype(BF16)
        weights = jnp.concatenate([proj, dec_buf[n]], axis=0)
        total += dot(weights, source[...], ((1,), (0,)))
    post = jnp.concatenate([post_ref[...]] * targets, axis=1)
    head_grad = (total[0:width] * post).astype(BF16)
    for r in range(targets):
        cols = slice(r * seq, (r + 1) * seq)
        mixed = jnp.zeros((head, seq), F32)
        for h in range(heads):
            mixed += dot(head_grad[h * head : (h + 1) * head, cols], patterns_ref[h], ((1,), (0,)))
        value_ref[cols, :] = mixed.T.astype(BF16)
    direct_ref[...] = total[width:].T


def score_kernel(geometry, value_ref, direct_ref, pre_ref, ids_ref, m0, m1, m2, m3, out_ref):
    targets, seq, nx, nzh, owners = geometry
    zh, zl = lax.axis_index("zh"), lax.axis_index("zl")
    value = value_ref[...]
    head = value.shape[1]
    slots = ids_ref.shape[0]
    lines = [ids_ref[...].astype(F32), pre_ref[...], jnp.zeros((7 - slots, seq), F32)]
    columns = jnp.concatenate(lines, axis=0).T
    ids = [columns[:, k : k + 1] for k in range(slots)]
    pre = columns[:, slots : slots + 1]
    totals = [[jnp.zeros((seq, BLK), F32) for _ in range(targets)] for _ in range(slots)]
    for turn, folded_ref in zip(TURNS, (m0, m1, m2, m3)):
        other = lax.rem(zl + 4 - turn, 4)
        shift = jnp.where(
            other == 0, nzh - 1, jnp.where(other == 1, 0, jnp.where(other == 2, 2, 1))
        )
        block = lax.rem(zh + shift, nzh)
        for x in range(nx):
            rows = folded_ref[:, x].reshape(BLK, head)
            scores = dot(value, rows, ((1,), (1,)))
            name = (x * nzh + block).astype(F32)
            for k in range(slots):
                hit = ids[k] == name
                for r in range(targets):
                    totals[k][r] += jnp.where(hit, scores[r * seq : (r + 1) * seq], 0.0)
    own = (lax.axis_index("x") * nzh + zh).astype(F32)
    direct = direct_ref[...]
    for k in range(slots):
        hit = ids[k] == own
        for r in range(targets):
            picked = jnp.where(hit, direct[r * seq : (r + 1) * seq], 0.0)
            totals[k][r] = totals[k][r] * pre + picked
    piece = seq // owners
    for i in range(owners):
        place = ORDER.index(i // nzh) * nzh + ORDER.index(i % nzh)
        for r in range(targets):
            both = [totals[k][r][i * piece : (i + 1) * piece] for k in range(slots)]
            out_ref[place, :, r * BLK : (r + 1) * BLK] = jnp.concatenate(both, axis=0).astype(BF16)


def last_kernel(targets, parts_ref, acts_ref, out_ref):
    total = jnp.sum(parts_ref[...].astype(F32), axis=0)
    acts = acts_ref[...].astype(F32)
    tokens = acts.shape[0]
    slots = acts.shape[1] // BLK
    for r in range(targets):
        for k in range(slots):
            cols = slice(k * BLK, (k + 1) * BLK)
            out_ref[r, :, cols] = (
                total[k * tokens : (k + 1) * tokens, r * BLK : (r + 1) * BLK] * acts[:, cols]
            )


def shards(
    sizes,
    grad_top,
    post_scale,
    post_gain,
    patterns,
    out_proj,
    value_proj,
    pre_scale,
    pre_gain,
    decoder,
    block_ids,
    feature_acts,
):
    nzl, ny, nc, nx, nzh = sizes
    owners = nx * nzh
    targets, seq, local = grad_top.shape
    rows = targets * seq
    heads, head = patterns.shape[0], out_proj.shape[0] // patterns.shape[0]
    width = out_proj.shape[1]
    chunk = width // nx
    slots = block_ids.shape[1]
    copies = ny * nc
    share = BLK // copies
    tokens = feature_acts.shape[0]
    vmem = pl.BlockSpec(memory_space=pltpu.VMEM)
    hbm = pl.BlockSpec(memory_space=pl.ANY)

    packed, weights, near = pl.pallas_call(
        functools.partial(front_kernel, share),
        in_specs=[hbm] * 5,
        out_shape=[
            jax.ShapeDtypeStruct((local + 16, rows), BF16),
            jax.ShapeDtypeStruct((heads * head + BLK, chunk), BF16),
            jax.ShapeDtypeStruct((share, width), BF16),
        ],
        scratch_shapes=[
            pltpu.VMEM((local,), BF16),
            pltpu.VMEM((local,), BF16),
            pltpu.SemaphoreType.DMA((5 + targets,)),
        ],
        compiler_params=FULL,
    )(grad_top.transpose(0, 2, 1), out_proj, decoder, post_gain, pre_gain)
    near = lax.ppermute(near, AXES, decoder_moves(sizes))
    weights = lax.ppermute(weights, "x", ring(nx, 2))
    columns = lax.all_gather(packed, "zh", axis=0, tiled=False)
    wide, gains = pl.pallas_call(
        join_kernel,
        out_shape=[
            jax.ShapeDtypeStruct((chunk, rows), BF16),
            jax.ShapeDtypeStruct((16, rows), BF16),
        ],
        compiler_params=PARAMS,
    )(columns)
    tail = jnp.pad(gains, ((0, share - 16), (0, 0)))
    near = lax.all_gather(jnp.concatenate([near, tail], axis=1), "x", axis=0, tiled=False)
    wide, near = lax.optimization_barrier((wide, near))
    left = lax.ppermute(wide, "x", ring(nx, 1))
    right = lax.ppermute(wide, "x", ring(nx, nx - 1))
    folded = pl.pallas_call(
        fold_kernel,
        grid=(nx,),
        in_specs=[
            pl.BlockSpec((nx, share, chunk), lambda i: (0, 0, i)),
            pl.BlockSpec((1, 16, rows), lambda i: (i, 0, width // rows)),
            pl.BlockSpec((head, chunk), lambda i: (0, i)),
        ],
        out_specs=pl.BlockSpec((copies, nx * share, head), lambda i: (0, 0, 0)),
        out_shape=jax.ShapeDtypeStruct((copies, nx * share, head), BF16),
        scratch_shapes=[pltpu.VMEM((nx * share, head), F32)],
        compiler_params=PARAMS,
    )(near, near, value_proj)
    wide, folded = lax.optimization_barrier((wide, folded))
    folded = lax.all_to_all(folded, ("c", "y"), 0, 0)
    far = pl.pallas_call(
        functools.partial(far_kernel, heads * head),
        out_shape=jax.ShapeDtypeStruct((heads * head + BLK, rows), BF16),
        compiler_params=PARAMS,
    )(wide, weights, gains)
    far = lax.ppermute(far, "x", ring(nx, 2))
    folded = folded.reshape(copies, nx, share, head)
    foldeds = [folded if k == 0 else lax.ppermute(folded, "zl", ring(nzl, k)) for k in TURNS]

    value, direct = pl.pallas_call(
        functools.partial(value_kernel, (targets, seq, heads, head)),
        in_specs=[vmem] * 4 + [hbm] * 3 + [vmem] * 2,
        out_specs=[vmem, vmem],
        out_shape=[
            jax.ShapeDtypeStruct((rows, head), BF16),
            jax.ShapeDtypeStruct((rows, BLK), F32),
        ],
        scratch_shapes=[
            pltpu.VMEM((nx, 16, rows), BF16),
            pltpu.VMEM((3, heads * head, chunk), BF16),
            pltpu.VMEM((3, BLK, chunk), BF16),
            pltpu.SemaphoreType.DMA,
            pltpu.SemaphoreType.DMA((2, 3)),
        ],
        compiler_params=PARAMS,
    )(wide, left, right, far, out_proj, decoder, near, post_scale[None, :], patterns)
    parts = pl.pallas_call(
        functools.partial(score_kernel, (targets, seq, nx, nzh, owners)),
        out_shape=jax.ShapeDtypeStruct((owners, slots * tokens, targets * BLK), BF16),
        compiler_params=PARAMS,
    )(value, direct, pre_scale[None, :], block_ids.T, *foldeds)

    group = [i * nzh + z for i in ORDER for z in ORDER]
    parts = lax.all_to_all(parts, TP, 0, 0, axis_index_groups=[group])
    return pl.pallas_call(
        functools.partial(last_kernel, targets),
        out_shape=jax.ShapeDtypeStruct((targets, tokens, slots * BLK), F32),
        compiler_params=PARAMS,
    )(parts, feature_acts)


def solution(mesh):
    sizes = (4, 4, mesh.devices.size // 256, 4, 4)
    mesh = Mesh(mesh.devices.reshape(sizes), AXES)
    in_specs = (
        P(GRP, None, TP),
        P(),
        P(TP),
        P(TP, None, None),
        P(TP, None),
        P(TP, None),
        P(),
        P(TP),
        P(TP, None),
        P(),
        P(TP, None),
    )
    return jax.shard_map(
        functools.partial(shards, sizes),
        mesh=mesh,
        in_specs=in_specs,
        out_specs=P(GRP, TP, None),
        check_vma=False,
    )
```

```python
import functools

import jax
import jax.numpy as jnp
from jax import lax
from jax.experimental import pallas as pl
from jax.experimental.pallas import tpu as pltpu
from jax.sharding import Mesh, PartitionSpec as P

BLK = 128
LANES = 128
AXES = ("zl", "y", "c", "x", "zh")
GRP = ("zl", "y", "c")
TP = ("x", "zh")
TURNS = (0, 1, 3, 2)
ORDER = (2, 3, 0, 1)
F32 = jnp.float32
BF16 = jnp.bfloat16
PARAMS = pltpu.CompilerParams(vmem_limit_bytes=40 * 1024 * 1024)
FULL = pltpu.CompilerParams(vmem_limit_bytes=60 * 1024 * 1024)


def source_block(zh, zl, n):
    return (zh + (n - 1, 0, 2, 1)[zl]) % n


def decoder_moves(sizes):
    nzl, ny, nc, nx, nzh = sizes
    senders = (nzl - 1, 2, 1, 0)
    at = lambda zl, y, c, x, zh: (((zl * ny + y) * nc + c) * nx + x) * nzh + zh
    return [
        (at(senders[zl], y, c, x, source_block(zh, zl, nzh)), at(zl, y, c, x, zh))
        for zl in range(nzl)
        for y in range(ny)
        for c in range(nc)
        for x in range(nx)
        for zh in range(nzh)
    ]


def ring(size, step):
    return [(i, (i + step) % size) for i in range(size)]


def dot(left, right, dims):
    return lax.dot_general(left, right, (dims, ((), ())), preferred_element_type=F32)


def front_kernel(share, top, out_proj, dec, post, pre, out_ref, far_ref, near_ref, flat0, flat1, sems):
    targets, local, seq = top.shape
    wide = targets * seq
    height, chunk = out_proj.shape[0], far_ref.shape[1]
    first = pl.multiple_of(lax.rem(lax.axis_index("x") + 2, 4) * chunk, LANES)
    cols = pl.ds(first, chunk)
    copies = [
        pltpu.make_async_copy(post, flat0, sems.at[0]),
        pltpu.make_async_copy(pre, flat1, sems.at[1]),
        pltpu.make_async_copy(out_proj.at[:, cols], far_ref.at[pl.ds(0, height), :], sems.at[2]),
        pltpu.make_async_copy(dec.at[:, cols], far_ref.at[pl.ds(height, BLK), :], sems.at[3]),
    ]
    rows = pl.ds(pl.multiple_of(lax.axis_index(("c", "y")) * share, share), share)
    copies.append(pltpu.make_async_copy(dec.at[rows, :], near_ref, sems.at[4 + targets]))
    for r in range(targets):
        place = out_ref.at[pl.ds(0, local), pl.ds(r * seq, seq)]
        copies.append(pltpu.make_async_copy(top.at[r], place, sems.at[4 + r]))
    for c in copies:
        c.start()
    for c in copies[:2]:
        c.wait()
    zh = lax.axis_index("zh")
    lane = lax.broadcasted_iota(jnp.int32, (8, wide), 1)
    line = lax.broadcasted_iota(jnp.int32, (8, wide), 0)
    both = []
    for ref in (flat0, flat1):
        flat = ref[...].astype(F32).reshape(1, local)
        flat = jnp.concatenate([flat, jnp.zeros((1, wide - local), F32)], axis=1)
        full = jnp.broadcast_to(flat, (8, wide))
        moved = full
        for z in range(1, 4):
            moved = jnp.where(zh == z, pltpu.roll(full, (z * local) % wide, 1), moved)
        place = line * wide + lane - zh * local
        both.append(jnp.where((place >= 0) & (place < local), moved, 0.0))
    out_ref[local:, :] = jnp.concatenate(both, axis=0).astype(BF16)
    for c in copies[2:]:
        c.wait()


def far_kernel(width, wide_ref, weights_ref, gain_ref, out_ref):
    gain = gain_row(gain_ref[...], 0, weights_ref.shape[1] // gain_ref.shape[1])
    proj = weights_ref[0:width] * gain.astype(BF16)
    weights = jnp.concatenate([proj, weights_ref[width:]], axis=0)
    out_ref[...] = dot(weights, wide_ref[...], ((1,), (0,))).astype(BF16)


def join_kernel(columns_ref, wide_ref, gain_ref):
    zone, tall, rows = columns_ref.shape
    local = tall - 16
    total = None
    for z in range(zone):
        wide_ref[z * local : (z + 1) * local] = columns_ref[z, 0:local]
        tail = columns_ref[z, local:].astype(F32)
        total = tail if total is None else total + tail
    gain_ref[...] = total.astype(BF16)


def gain_row(tile, first, count):
    tile = tile.astype(F32)
    return jnp.concatenate([tile[first + i : first + i + 1] for i in range(count)], axis=1)


def fold_kernel(near_ref, value_ref, out_ref):
    senders, share, tall = near_ref.shape
    width = value_ref.shape[1]
    chunk, wide = width // senders, tall - width
    total = None
    for i in range(senders):
        cols = slice(i * chunk, (i + 1) * chunk)
        gain = gain_row(near_ref[i, 0:16, width:], 8, chunk // wide).astype(BF16)
        dec = near_ref[:, :, cols].reshape(senders * share, chunk) * gain
        part = dot(dec, value_ref[:, cols], ((1,), (1,)))
        total = part if total is None else total + part
    out_ref[...] = jnp.broadcast_to(total.astype(BF16)[None], out_ref.shape)


def value_kernel(
    geometry,
    own,
    left,
    right,
    far,
    out_proj,
    decoder,
    near,
    post_ref,
    patterns_ref,
    value_ref,
    direct_ref,
    gains_ref,
    proj_buf,
    dec_buf,
    sem,
    sems,
):
    targets, seq, heads, head = geometry
    width = heads * head
    chunk = proj_buf.shape[2]
    size = 4
    mine = lax.axis_index("x")
    places = [lax.rem(mine + size - turn, size) for turn in (0, 1, 3)]
    tail = pl.ds(decoder.shape[1], gains_ref.shape[2])
    fetch = pltpu.make_async_copy(near.at[:, pl.ds(0, 16), tail], gains_ref, sem)
    fetch.start()
    copies = []
    for n, place in enumerate(places):
        cols = pl.ds(pl.multiple_of(place * chunk, LANES), chunk)
        group = [
            pltpu.make_async_copy(out_proj.at[:, cols], proj_buf.at[n], sems.at[0, n]),
            pltpu.make_async_copy(decoder.at[:, cols], dec_buf.at[n], sems.at[1, n]),
        ]
        for c in group:
            c.start()
        copies.append(group)
    fetch.wait()
    total = far[...].astype(F32)
    for n, source in enumerate((own, left, right)):
        for c in copies[n]:
            c.wait()
        gain = gain_row(gains_ref[places[n]], 0, chunk // gains_ref.shape[2])
        proj = proj_buf[n] * gain.astype(BF16)
        weights = jnp.concatenate([proj, dec_buf[n]], axis=0)
        total += dot(weights, source[...], ((1,), (0,)))
    post = jnp.concatenate([post_ref[...]] * targets, axis=1)
    head_grad = (total[0:width] * post).astype(BF16)
    for r in range(targets):
        cols = slice(r * seq, (r + 1) * seq)
        mixed = jnp.zeros((head, seq), F32)
        for h in range(heads):
            mixed += dot(head_grad[h * head : (h + 1) * head, cols], patterns_ref[h], ((1,), (0,)))
        value_ref[cols, :] = mixed.T.astype(BF16)
    direct_ref[...] = total[width:].T


def score_kernel(geometry, value_ref, direct_ref, pre_ref, ids_ref, m0, m1, m2, m3, out_ref):
    targets, seq, nx, nzh, owners = geometry
    zh, zl = lax.axis_index("zh"), lax.axis_index("zl")
    value = value_ref[...]
    head = value.shape[1]
    slots = ids_ref.shape[0]
    lines = [ids_ref[...].astype(F32), pre_ref[...], jnp.zeros((7 - slots, seq), F32)]
    columns = jnp.concatenate(lines, axis=0).T
    ids = [columns[:, k : k + 1] for k in range(slots)]
    pre = columns[:, slots : slots + 1]
    totals = [[jnp.zeros((seq, BLK), F32) for _ in range(targets)] for _ in range(slots)]
    for turn, folded_ref in zip(TURNS, (m0, m1, m2, m3)):
        other = lax.rem(zl + 4 - turn, 4)
        shift = jnp.where(
            other == 0, nzh - 1, jnp.where(other == 1, 0, jnp.where(other == 2, 2, 1))
        )
        block = lax.rem(zh + shift, nzh)
        for x in range(nx):
            rows = folded_ref[:, x].reshape(BLK, head)
            scores = dot(value, rows, ((1,), (1,)))
            name = (x * nzh + block).astype(F32)
            for k in range(slots):
                hit = ids[k] == name
                for r in range(targets):
                    totals[k][r] += jnp.where(hit, scores[r * seq : (r + 1) * seq], 0.0)
    own = (lax.axis_index("x") * nzh + zh).astype(F32)
    direct = direct_ref[...]
    for k in range(slots):
        hit = ids[k] == own
        for r in range(targets):
            picked = jnp.where(hit, direct[r * seq : (r + 1) * seq], 0.0)
            totals[k][r] = totals[k][r] * pre + picked
    piece = seq // owners
    for i in range(owners):
        place = ORDER.index(i // nzh) * nzh + ORDER.index(i % nzh)
        for r in range(targets):
            both = [totals[k][r][i * piece : (i + 1) * piece] for k in range(slots)]
            out_ref[place, :, r * BLK : (r + 1) * BLK] = jnp.concatenate(both, axis=0).astype(BF16)


def last_kernel(targets, parts_ref, acts_ref, out_ref):
    total = jnp.sum(parts_ref[...].astype(F32), axis=0)
    acts = acts_ref[...].astype(F32)
    tokens = acts.shape[0]
    slots = acts.shape[1] // BLK
    for r in range(targets):
        for k in range(slots):
            cols = slice(k * BLK, (k + 1) * BLK)
            out_ref[r, :, cols] = (
                total[k * tokens : (k + 1) * tokens, r * BLK : (r + 1) * BLK] * acts[:, cols]
            )


def shards(
    sizes,
    grad_top,
    post_scale,
    post_gain,
    patterns,
    out_proj,
    value_proj,
    pre_scale,
    pre_gain,
    decoder,
    block_ids,
    feature_acts,
):
    nzl, ny, nc, nx, nzh = sizes
    owners = nx * nzh
    targets, seq, local = grad_top.shape
    rows = targets * seq
    heads, head = patterns.shape[0], out_proj.shape[0] // patterns.shape[0]
    width = out_proj.shape[1]
    chunk = width // nx
    slots = block_ids.shape[1]
    copies = ny * nc
    share = BLK // copies
    tokens = feature_acts.shape[0]
    vmem = pl.BlockSpec(memory_space=pltpu.VMEM)
    hbm = pl.BlockSpec(memory_space=pl.ANY)

    packed, weights, near = pl.pallas_call(
        functools.partial(front_kernel, share),
        in_specs=[hbm] * 5,
        out_shape=[
            jax.ShapeDtypeStruct((local + 16, rows), BF16),
            jax.ShapeDtypeStruct((heads * head + BLK, chunk), BF16),
            jax.ShapeDtypeStruct((share, width), BF16),
        ],
        scratch_shapes=[
            pltpu.VMEM((local,), BF16),
            pltpu.VMEM((local,), BF16),
            pltpu.SemaphoreType.DMA((5 + targets,)),
        ],
        compiler_params=FULL,
    )(grad_top.transpose(0, 2, 1), out_proj, decoder, post_gain, pre_gain)
    near = lax.ppermute(near, AXES, decoder_moves(sizes))
    weights = lax.ppermute(weights, "x", ring(nx, 2))
    columns = lax.all_gather(packed, "zh", axis=0, tiled=False)
    wide, gains = pl.pallas_call(
        join_kernel,
        out_shape=[
            jax.ShapeDtypeStruct((chunk, rows), BF16),
            jax.ShapeDtypeStruct((16, rows), BF16),
        ],
        compiler_params=PARAMS,
    )(columns)
    tail = jnp.pad(gains, ((0, share - 16), (0, 0)))
    near = lax.all_gather(jnp.concatenate([near, tail], axis=1), "x", axis=0, tiled=False)
    wide, near = lax.optimization_barrier((wide, near))
    left = lax.ppermute(wide, "x", ring(nx, 1))
    right = lax.ppermute(wide, "x", ring(nx, nx - 1))
    folded = pl.pallas_call(
        fold_kernel,
        out_shape=jax.ShapeDtypeStruct((copies, nx * share, head), BF16),
        compiler_params=PARAMS,
    )(near, value_proj)
    wide, folded = lax.optimization_barrier((wide, folded))
    folded = lax.all_to_all(folded, ("c", "y"), 0, 0)
    far = pl.pallas_call(
        functools.partial(far_kernel, heads * head),
        out_shape=jax.ShapeDtypeStruct((heads * head + BLK, rows), BF16),
        compiler_params=PARAMS,
    )(wide, weights, gains)
    far = lax.ppermute(far, "x", ring(nx, 2))
    folded = folded.reshape(copies, nx, share, head)
    foldeds = [folded if k == 0 else lax.ppermute(folded, "zl", ring(nzl, k)) for k in TURNS]

    value, direct = pl.pallas_call(
        functools.partial(value_kernel, (targets, seq, heads, head)),
        in_specs=[vmem] * 4 + [hbm] * 3 + [vmem] * 2,
        out_specs=[vmem, vmem],
        out_shape=[
            jax.ShapeDtypeStruct((rows, head), BF16),
            jax.ShapeDtypeStruct((rows, BLK), F32),
        ],
        scratch_shapes=[
            pltpu.VMEM((nx, 16, rows), BF16),
            pltpu.VMEM((3, heads * head, chunk), BF16),
            pltpu.VMEM((3, BLK, chunk), BF16),
            pltpu.SemaphoreType.DMA,
            pltpu.SemaphoreType.DMA((2, 3)),
        ],
        compiler_params=PARAMS,
    )(wide, left, right, far, out_proj, decoder, near, post_scale[None, :], patterns)
    parts = pl.pallas_call(
        functools.partial(score_kernel, (targets, seq, nx, nzh, owners)),
        out_shape=jax.ShapeDtypeStruct((owners, slots * tokens, targets * BLK), BF16),
        compiler_params=PARAMS,
    )(value, direct, pre_scale[None, :], block_ids.T, *foldeds)

    group = [i * nzh + z for i in ORDER for z in ORDER]
    parts = lax.all_to_all(parts, TP, 0, 0, axis_index_groups=[group])
    return pl.pallas_call(
        functools.partial(last_kernel, targets),
        out_shape=jax.ShapeDtypeStruct((targets, tokens, slots * BLK), F32),
        compiler_params=PARAMS,
    )(parts, feature_acts)


def solution(mesh):
    sizes = (4, 4, mesh.devices.size // 256, 4, 4)
    mesh = Mesh(mesh.devices.reshape(sizes), AXES)
    in_specs = (
        P(GRP, None, TP),
        P(),
        P(TP),
        P(TP, None, None),
        P(TP, None),
        P(TP, None),
        P(),
        P(TP),
        P(TP, None),
        P(),
        P(TP, None),
    )
    return jax.shard_map(
        functools.partial(shards, sizes),
        mesh=mesh,
        in_specs=in_specs,
        out_specs=P(GRP, TP, None),
        check_vma=False,
    )
```
